256 devices in a mesh: blk: 32 (over z, y), fsdp: 8 (over x, core).
Axes of the slice: x: 4, y: 4, z: 8, core: 2. Of those that a mesh axis runs over, the one named last changes fastest.
Arguments:
- tokens: bfloat16 [32768, 512], P('blk'), may hold values from -6 to 6
- cotangent: bfloat16 [32768, 512], P('blk'), may hold values from -6 to 6
- in_gain: float32 [2, 512], replicated, may hold values from 0.5 to 1.5
- w_pair: bfloat16 [2, 2, 512, 1024], P(None, None, None, 'fsdp'), may hold values from -0.25 to 0.25
- w_shared: bfloat16 [2, 512, 256], P(None, 'fsdp'), may hold values from -0.25 to 0.25
- w_step: bfloat16 [2, 512, 16], P(None, None, 'fsdp'), may hold values from -0.25 to 0.25
- step_bias: float32 [2, 16], P(None, 'fsdp'), may hold values from -2 to 0
- conv_values: float32 [2, 4, 1024], P(None, None, 'fsdp'), may hold values from -3 to 3
- conv_shared: float32 [2, 4, 256], replicated, may hold values from -3 to 3
- log_decay: float32 [2, 16, 32768], P(None, 'fsdp', 'blk'), may hold values from -1.5 to 0, as said below
- skip_gain: float32 [2, 16], P(None, 'fsdp'), may hold values from 0.5 to 1.5
- out_gain: float32 [2, 1024], P(None, 'fsdp'), may hold values from 0.5 to 1.5
- w_out: bfloat16 [2, 1024, 512], P(None, 'fsdp'), may hold values from -0.1875 to 0.1875
Outputs:
- mixed: bfloat16 [32768, 512], P('blk')
- grad_tokens: bfloat16 [32768, 512], P('blk')
The draws below stay inside these ranges and needn't reach their ends.
Inputs may be any that keep to these rules, and one draw needn't show every extreme that they name: `log_decay`: natural logarithm of a decay factor, negative.
All inputs are finite; a program needn't handle non-finite values.
Results may differ from the reference program's by a relative error of at most 0.025.
Values may be sent and summed in bfloat16 or wider, within the bound.
A program may use at most 384 MiB of HBM per device.

```python
import math
from functools import partial
import jax
import jax.numpy as jnp
from jax import lax

D = 512
H = 16
HEAD = 64
STATE = 128
CONV = 4
BLOCK = 128
LAYERS = 2
TOKENS = 32768
N_FSDP = 8


def draw_log_decay(key, part):
    key = jax.random.fold_in(key, 7)
    subkeys = jax.random.split(key, 6)
    portion = 0.5
    head_shape = (LAYERS, H, 1)
    slower = -jax.random.uniform(subkeys[0], head_shape, jnp.float32, 0.15, 0.45) / TOKENS
    faster = -jax.random.uniform(subkeys[1], head_shape, jnp.float32, 1.0 / 50.0, 1.0 / 30.0)
    chosen = jax.random.uniform(subkeys[2], head_shape, jnp.float32) < portion
    reference_speed = jnp.where(chosen, faster, slower)
    scaling_coefficient = jnp.exp(jax.random.uniform(subkeys[3], (LAYERS, H, TOKENS // BLOCK, 1), jnp.float32, math.log(0.5), math.log(2.0)))
    scaling_coefficient = jnp.broadcast_to(scaling_coefficient, (LAYERS, H, TOKENS // BLOCK, BLOCK)).reshape(LAYERS, H, TOKENS)
    cell_locations = jax.random.randint(subkeys[4], (LAYERS, H, 2, 1), 0, TOKENS)
    objective_scores = jax.random.uniform(subkeys[5], (LAYERS, H, 2, 1), jnp.float32, 0.22, 0.69)
    ordering_indices = jnp.arange(TOKENS, dtype=jnp.int32)[None, None, None, :]
    clustered_batches = jnp.sum(jnp.where(cell_locations == ordering_indices, objective_scores, 0.0), axis=2)
    return reference_speed * scaling_coefficient - clustered_batches


def level_of(key, shape, cuts, least, top_value):
    loudness = 1.0
    for axis_at, shards_of in cuts:
        draws = jax.random.uniform(jax.random.fold_in(jax.random.fold_in(key, 6), axis_at), (shards_of,), jnp.float32, least / len(cuts), top_value / len(cuts))
        loudness = loudness * jnp.repeat(jnp.exp(draws), shape[axis_at] // shards_of).reshape((-1,) + (1,) * (len(shape) - 1 - axis_at))
    return loudness


def centred(rng, extent, scale, most, cuts=(), held_as=jnp.bfloat16):
    entries = scale * jax.random.normal(rng, extent, jnp.float32)
    if cuts:
        entries = entries * level_of(rng, extent, cuts, -0.22, 0.18)
    return jnp.clip(entries, -most, most).astype(held_as)


def setup_inputs(seed: int = 0) -> dict:
    streams_of = jax.random.split(jax.random.key(seed), 14)
    tokens = centred(streams_of[0], (TOKENS, D), 1.0, 6.0, ((0, 32),))
    cotangent = centred(streams_of[1], (TOKENS, D), 1.0, 6.0, ((0, 32),))
    in_gain = jnp.clip(1.0 + 0.1 * jax.random.normal(streams_of[2], (LAYERS, D), jnp.float32), 0.5, 1.5)
    w_pair = centred(streams_of[3], (LAYERS, 2, D, H * HEAD), D ** -0.5, 0.25, ((3, 8),))
    w_shared = centred(streams_of[4], (LAYERS, D, 2 * STATE), D ** -0.5, 0.25, ((1, 8),))
    w_step = centred(streams_of[5], (LAYERS, D, H), D ** -0.5, 0.25, ((2, 8),))
    step_bias = jnp.clip(-2.0 + 2.0 * jax.random.uniform(streams_of[6], (LAYERS, H), jnp.float32) ** level_of(streams_of[6], (LAYERS, H), ((1, 8),), -0.2, 0.2), -2.0, 0.0)
    conv_values = centred(streams_of[7], (LAYERS, CONV, H * HEAD), CONV ** -0.5, 3.0, ((2, 8),), jnp.float32)
    conv_shared = centred(streams_of[8], (LAYERS, CONV, 2 * STATE), CONV ** -0.5, 3.0, (), jnp.float32)
    log_decay = draw_log_decay(jax.random.fold_in(streams_of[13], 71), 0)
    skip_gain = jnp.clip(0.5 + 1.0 * jax.random.uniform(streams_of[10], (LAYERS, H), jnp.float32) ** level_of(streams_of[10], (LAYERS, H), ((1, 8),), -0.2, 0.2), 0.5, 1.5)
    out_gain = jnp.clip(1.0 + 0.1 * jax.random.normal(streams_of[11], (LAYERS, H * HEAD), jnp.float32), 0.5, 1.5)
    w_out = centred(streams_of[12], (LAYERS, H * HEAD, D), (H * HEAD) ** -0.5, 0.1875, ((1, 8),))
    return {"tokens": tokens, "cotangent": cotangent, "in_gain": in_gain, "w_pair": w_pair, "w_shared": w_shared, "w_step": w_step, "step_bias": step_bias, "conv_values": conv_values, "conv_shared": conv_shared, "log_decay": log_decay, "skip_gain": skip_gain, "out_gain": out_gain, "w_out": w_out}


tiny_offset = 1e-05
highest = lax.Precision.HIGHEST

def norm_input(stream, gain):
    return stream * lax.rsqrt(lax.optimization_barrier(jnp.mean(stream * stream, axis=-1, keepdims=True)) + tiny_offset) * gain

def project(normed, w_pair, w_shared, w_step, step_bias):
    hidden = normed.astype(jnp.bfloat16)
    values = jnp.dot(hidden, w_pair[0], preferred_element_type=jnp.float32).astype(jnp.bfloat16)
    shared = jnp.dot(hidden, w_shared, preferred_element_type=jnp.float32).astype(jnp.bfloat16)
    gates = jnp.dot(hidden, w_pair[1], preferred_element_type=jnp.float32).astype(jnp.bfloat16)
    step_size = jax.nn.softplus(jnp.dot(hidden, w_step, preferred_element_type=jnp.float32) + step_bias)
    before, gates = lax.optimization_barrier((jnp.concatenate([values, shared], axis=1), gates))
    return (before.astype(jnp.float32), gates.astype(jnp.float32), step_size)

def conv_act(rim_rows, before, kernel):
    length = before.shape[0]
    joined = jnp.concatenate([rim_rows, before], axis=0)
    total = kernel[0] * joined[0:length]
    for offset in range(1, kernel.shape[0]):
        total = total + kernel[offset] * joined[offset:offset + length]
    active = lax.optimization_barrier(jax.nn.silu(total).astype(jnp.bfloat16))
    return active.astype(jnp.float32)

def block_step(state, pieces):
    values, inputs_b, outputs_c, step_size, log_rate = pieces
    length = log_rate.shape[0]
    cumulative_tally = jnp.cumsum(log_rate, axis=0)
    gaps = cumulative_tally[:, None, :] - cumulative_tally[None, :, :]
    later = lax.broadcasted_iota(jnp.int32, (length, length), 0) >= lax.broadcasted_iota(jnp.int32, (length, length), 1)
    decay = jnp.exp(jnp.where(later[:, :, None], gaps, -1e+30))
    scores = jnp.einsum('tn,sn->ts', outputs_c, inputs_b, precision=highest)
    scaled = values * step_size[:, :, None]
    result = jnp.einsum('tsh,shp->thp', decay * scores[:, :, None], scaled, precision=highest)
    result = result + jnp.exp(cumulative_tally)[:, :, None] * jnp.einsum('tn,hpn->thp', outputs_c, state, precision=highest)
    remain = jnp.exp(cumulative_tally[-1][None, :] - cumulative_tally)
    state = jnp.exp(cumulative_tally[-1])[:, None, None] * state + jnp.einsum('sh,shp,sn->hpn', remain, scaled, inputs_b, precision=highest)
    return (state, result)

def ssd_scan(values, inputs_b, outputs_c, step_size, log_rate, state):
    length = log_rate.shape[0]
    heads = log_rate.shape[1]
    count = length // BLOCK
    pieces = (values.reshape(count, BLOCK, heads, HEAD), inputs_b.reshape(count, BLOCK, STATE), outputs_c.reshape(count, BLOCK, STATE), step_size.reshape(count, BLOCK, heads), log_rate.reshape(count, BLOCK, heads))
    state, result = lax.scan(block_step, state, pieces)
    return (state, result.reshape(length, heads, HEAD))

def split_active(active, heads):
    values = active[:, :heads * HEAD].reshape(active.shape[0], heads, HEAD)
    inputs_b = active[:, heads * HEAD:heads * HEAD + STATE]
    outputs_c = active[:, heads * HEAD + STATE:]
    return (values, inputs_b, outputs_c)

def gate_out(mixed_y, gates, gain, w_out):
    length, heads = (mixed_y.shape[0], mixed_y.shape[1])
    gated = mixed_y * jax.nn.silu(gates).reshape(length, heads, HEAD)
    normed = gated * lax.rsqrt(lax.optimization_barrier(jnp.mean(gated * gated, axis=-1, keepdims=True)) + tiny_offset) * gain.reshape(heads, HEAD)
    return jnp.dot(normed.reshape(length, heads * HEAD).astype(jnp.bfloat16), w_out, preferred_element_type=jnp.float32)

def group_branch(normed, w_pair, w_shared, w_step, step_bias, kernel, log_rate, skip_gain, gain, w_out):
    heads = log_rate.shape[1]
    before, gates, step_size = project(normed, w_pair, w_shared, w_step, step_bias)
    rim_rows = jnp.zeros((CONV - 1, before.shape[1]), jnp.float32)
    active = conv_act(rim_rows, before, kernel)
    values, inputs_b, outputs_c = split_active(active, heads)
    state = jnp.zeros((heads, HEAD, STATE), jnp.float32)
    closing, mixed_y = ssd_scan(values, inputs_b, outputs_c, step_size, log_rate, state)
    mixed_y = mixed_y + skip_gain[None, :, None] * values
    return gate_out(mixed_y, gates, gain, w_out)

def reference(tokens, cotangent, in_gain, w_pair, w_shared, w_step, step_bias, conv_values, conv_shared, log_decay, skip_gain, out_gain, w_out):
    groups = N_FSDP
    width = H // groups
    stream = tokens
    saved = []
    for layer_id in range(LAYERS):
        current = stream.astype(jnp.float32)
        normed, norm_back = jax.vjp(partial(norm_input, gain=in_gain[layer_id]), current)
        total = jnp.zeros(current.shape, jnp.float32)
        backs = []
        for group in range(groups):
            first = group * width
            last = first + width
            kernel = jnp.concatenate([conv_values[layer_id][:, first * HEAD:last * HEAD], conv_shared[layer_id]], axis=1)
            branch_fn = partial(group_branch, w_pair=w_pair[layer_id][:, :, first * HEAD:last * HEAD], w_shared=w_shared[layer_id], w_step=w_step[layer_id][:, first:last], step_bias=step_bias[layer_id][first:last], kernel=kernel, log_rate=log_decay[layer_id][first:last].T, skip_gain=skip_gain[layer_id][first:last], gain=out_gain[layer_id][first * HEAD:last * HEAD], w_out=w_out[layer_id][first * HEAD:last * HEAD])
            piece, back = jax.vjp(branch_fn, normed)
            total = total + piece
            backs.append(back)
        stream = (current + total).astype(jnp.bfloat16)
        saved.append((norm_back, backs))
    upstream = cotangent
    for layer_id in reversed(range(LAYERS)):
        norm_back, backs = saved[layer_id]
        incoming = upstream.astype(jnp.float32)
        grad_normed = jnp.zeros(incoming.shape, jnp.float32)
        for back in backs:
            grad_normed = grad_normed + back(incoming)[0]
        upstream = (incoming + norm_back(grad_normed)[0]).astype(jnp.bfloat16)
    return (stream, upstream)
```

```python
import functools

import jax
import jax.numpy as jnp
from jax import lax
from jax.experimental import pallas as pl
from jax.experimental.pallas import tpu as pltpu
from jax.sharding import PartitionSpec as P

D = 512
H = 16
HEAD = 64
N = 128
T = 128
HP = H * HEAD
AC = HP + 2 * N
EPS = 1e-5
PY = 4
R2 = 8
F32, BF = jnp.float32, jnp.bfloat16
MESH = pl.DeviceIdType.MESH


def mm(a, b):
    return jnp.dot(a, b, preferred_element_type=F32)


def mmt(a, b):
    return lax.dot_general(a, b, (((1,), (1,)), ((), ())), preferred_element_type=F32)


def sigmoid(v):
    return 1.0 / (1.0 + jnp.exp(-v))


def iota(shape, dim):
    return lax.broadcasted_iota(jnp.int32, shape, dim)


def loop(count, fn):
    def step(i, carry):
        fn(i)
        return carry

    lax.fori_loop(0, count, step, 0)


def layout(nb, nf):
    ny, nz = PY, nb // PY
    np_ = ny * nf
    ar, lw = N // nf, HP // ny
    slots = nf * R2
    vm = pltpu.VMEM
    dma = pltpu.SemaphoreType.DMA
    return dict(
        Wv=vm((2, D, HP), BF), Wg=vm((2, D, HP), BF), Wo=vm((2, HP, D), BF), Ws=vm((2, D, 2 * N), BF),
        K1=vm((2, 8, HP), F32), K2=vm((slots, D + 128), F32), LR=vm((slots, T), F32),
        WST=vm((slots, D), BF), BIAS=vm((8, slots), F32), E=vm((2, slots, HP), BF), ET=vm((2, HP, slots), BF),
        J=vm((256, 256), BF), EC=vm((2, T, HP), F32), RM=vm((2, T, HP), F32),
        DM=vm((2, H, T, T), BF), DTM=vm((2, H, T, T), BF),
        SPS=vm((8, HP), F32), SPR=vm((np_, 8, lw), F32), EA=vm((2, np_, ar, lw), F32),
        ZS=vm((8, lw), F32), ZR=vm((nz, 8, lw), F32), EZ=vm((2, nz, ar, lw), F32),
        TOK=vm((T, D), BF), COT=vm((T, D), BF), MIXS=vm((T, D), BF), GRS=vm((T, D), BF),
        CUR=vm((2, T, D), F32), HID=vm((T, D), BF), BEF=vm((2, T + 8, AC), F32), DSIL=vm((2, T, AC), F32),
        ACT=vm((2, T, AC), BF), ST=vm((2, T, HP), F32), SGM=vm((2, T, slots), F32),
        XS=vm((2, T, HP), BF), WX=vm((2, T, HP), BF), BT=vm((N, T), BF), CT=vm((2, N, T), BF),
        SS=vm((T, T), F32), STT=vm((2, T, T), F32), SG=vm((T, HP), F32), DSG=vm((T, HP), F32), Y=vm((T, HP), F32),
        HO=vm((T, HP), BF), GN=vm((2, T, HP), F32), RSG=vm((2, T, HP), F32), RYD=vm((2, T, HP), F32),
        CL=vm((4, N, HP), BF), R1=vm((4, np_, ar, lw), BF), ZT=vm((4, ar, lw), BF), RZ=vm((4, nz, ar, lw), BF),
        SB=vm((4, np_, ar, lw), BF), OP=vm((4, N, HP), BF),
        DY=vm((T, HP), F32), Q=vm((T, HP), BF), DGA=vm((T, HP), BF), DXS=vm((T, HP), F32), DS=vm((T, T), F32),
        DBC=vm((T, 2 * N), F32), DST=vm((T, slots), F32), DTOT=vm((2, T + 8, AC), F32), DB=vm((T, AC), BF),
        DH=vm((T, D), F32), U=vm((T, D), F32),
        s_in=dma((2,)), s_small=dma((3,)), s_small_tx=dma((3,)), s_w=dma((2, 4, 3)), s_sib=dma((2, 4)), s_wloc=dma((2, 4)),
        s_w_tx=dma((2, 4)), s_sp=dma((2,)), s_sp_tx=dma((2,)), s_rim=dma((4,)), s_rim_tx=dma((4,)),
        s_a=dma((4,)), s_a_tx=dma((4,)), s_z=dma((4,)), s_z_tx=dma((4,)), s_b=dma((4,)), s_b_tx=dma((4,)),
        s_out=dma((2,)), s_out_tx=dma((2,)),
    )


class Refs:
    pass


def kernel(nb, nf, names, *refs):
    (tokens, cot, in_gain, w_pair, w_shared, w_out, pack1, pack2, lrp, conv_shared, mixed_o, grad_o) = refs[:12]
    r = Refs()
    for name, ref in zip(names, refs[12:]):
        setattr(r, name, ref)
    ny, nz = PY, nb // PY
    np_ = ny * nf
    ar, lw = N // nf, HP // ny
    slots = nf * R2
    hf = H // nf
    hf_bits = hf.bit_length() - 1
    cw = HP // nf
    nx = nf // 2
    blk, f = lax.axis_index("blk"), lax.axis_index("fsdp")
    z, y = blk // ny, blk % ny
    me = y * nf + f
    x, core = f // 2, f % 2

    def plane(q):
        return (z * ny + q // nf, q % nf)

    def remote(src, dst, tx, rx, dev):
        return pltpu.make_async_remote_copy(
            src_ref=src, dst_ref=dst, send_sem=tx, recv_sem=rx, device_id=dev, device_id_type=MESH
        )

    def arrived(ref, sem):
        pltpu.make_async_copy(ref, ref, sem).wait()

    def slot(l, h):
        return (h // hf) * R2 + l * hf + h % hf

    own = pl.ds(pl.multiple_of(f * T, T), T)
    in_tok = pltpu.make_async_copy(tokens.at[own, :], r.TOK, r.s_in.at[0])
    in_cot = pltpu.make_async_copy(cot.at[own, :], r.COT, r.s_in.at[1])
    in_tok.start()
    in_cot.start()

    cols = pl.ds(pl.multiple_of(f * cw, cw), cw)
    rows8 = pl.ds(pl.multiple_of(f * R2, R2), R2)
    pltpu.make_async_copy(pack1, r.K1.at[:, :, cols], r.s_small.at[0]).start()
    pltpu.make_async_copy(pack2, r.K2.at[rows8, :], r.s_small.at[1]).start()
    pltpu.make_async_copy(lrp.at[f], r.LR.at[rows8, :], r.s_small.at[2]).start()

    def send_small(k):
        g = (f + k) % nf
        dev = (blk, g)
        remote(lrp.at[g], r.LR.at[rows8, :], r.s_small_tx.at[2], r.s_small.at[2], dev).start()
        remote(pack1, r.K1.at[:, :, cols], r.s_small_tx.at[0], r.s_small.at[0], dev).start()
        remote(pack2, r.K2.at[rows8, :], r.s_small_tx.at[1], r.s_small.at[1], dev).start()

    lax.fori_loop(1, nf, lambda k, c: (send_small(k), c)[1], 0)

    def weight_src(l, a):
        return [w_shared.at[l], w_pair.at[l, 0], w_pair.at[l, 1], w_out.at[l]][a]

    def weight_dst(l, a, g, count=1):
        if a == 0:
            m = D // nf
            return r.Ws.at[l, pl.ds(pl.multiple_of(g * m, m), m * count), :]
        if a == 3:
            return r.Wo.at[l, pl.ds(pl.multiple_of(g * cw, cw), cw * count), :]
        return (r.Wv if a == 1 else r.Wg).at[l, :, pl.ds(pl.multiple_of(g * cw, cw), cw * count)]

    sibling = (blk, x * 2 + 1 - core)

    def weights_send(l, arrays):
        for a in arrays:
            mine = weight_dst(l, a, f)
            pltpu.make_async_copy(weight_src(l, a), mine, r.s_wloc.at[l, a]).start()
            for dx in range(1, nx):
                dev = (blk, ((x + dx) % nx) * 2 + core)
                remote(weight_src(l, a), mine, r.s_w_tx.at[l, a], r.s_w.at[l, a, dx - 1], dev).start()
            remote(weight_src(l, a), mine, r.s_w_tx.at[l, a], r.s_sib.at[l, a], sibling).start()

    def weights_forward(l, arrays):
        for a in arrays:
            for dx in range(1, nx):
                g = ((x + nx - dx) % nx) * 2 + core
                part = weight_dst(l, a, g)
                arrived(part, r.s_w.at[l, a, dx - 1])
                remote(part, part, r.s_w_tx.at[l, a], r.s_sib.at[l, a], sibling).start()

    def weights_wait(l, arrays):
        for a in arrays:
            pltpu.make_async_copy(weight_src(l, a), weight_dst(l, a, f), r.s_wloc.at[l, a]).wait()
            arrived(weight_dst(l, a, 0, nx), r.s_sib.at[l, a])

    weights_send(0, (0, 1, 2, 3))

    for l in range(2):
        s_at = iota((slots, HP), 0)
        head = iota((slots, HP), 1) >> 6
        want = (head >> hf_bits) * R2 + l * hf + (head & (hf - 1))
        r.E[l] = jnp.where(s_at == want, 1.0, 0.0).astype(BF)
        s_at = iota((HP, slots), 1)
        head = iota((HP, slots), 0) >> 6
        want = (head >> hf_bits) * R2 + l * hf + (head & (hf - 1))
        r.ET[l] = jnp.where(s_at == want, 1.0, 0.0).astype(BF)
    r.J[...] = jnp.where((iota((256, 256), 0) >> 6) == (iota((256, 256), 1) >> 6), 1.0 / HEAD, 0.0).astype(BF)

    def expand(v, l, at):
        hi = v.astype(BF)
        rest = v - hi.astype(F32)
        mid = rest.astype(BF)
        lo = (rest - mid.astype(F32)).astype(BF)
        e = r.E[l, :, at]
        return mm(hi, e) + mm(mid, e) + mm(lo, e)

    arrived(r.LR, r.s_small.at[2])
    upper = jnp.where(iota((T, T), 0) <= iota((T, T), 1), 1.0, 0.0)
    cum = jnp.dot(r.LR[...], upper, preferred_element_type=F32, precision=lax.Precision.HIGHEST)
    cum_t = jnp.transpose(cum)
    spans = [expand(cum_t[T - 8 :, :], l, slice(None))[7:8, :] for l in range(2)]
    r.SPS[...] = jnp.where(iota((8, HP), 0) < 4, spans[0], spans[1])

    def lanes_of(q):
        return pl.ds(pl.multiple_of((q // nf) * lw, lw), lw)

    def rows_of(q):
        return pl.ds(pl.multiple_of((q % nf) * ar, ar), ar)

    pltpu.make_async_copy(r.SPS.at[:, lanes_of(me)], r.SPR.at[me], r.s_sp.at[0]).start()

    def send_span(k):
        q = (me + k) % np_
        remote(r.SPS.at[:, lanes_of(q)], r.SPR.at[me], r.s_sp_tx.at[0], r.s_sp.at[0], plane(q)).start()

    lax.fori_loop(1, np_, lambda k, c: (send_span(k), c)[1], 0)

    ecum = jnp.exp(cum_t)
    remain = jnp.exp(cum_t[T - 1 :, :] - cum_t)
    for l in range(2):
        for j in range(4):
            at = pl.ds(j * 256, 256)
            r.EC[l, :, at] = expand(ecum, l, at)
            r.RM[l, :, at] = expand(remain, l, at)
    causal = iota((T, T), 0) >= iota((T, T), 1)
    anti = iota((T, T), 0) <= iota((T, T), 1)
    for l in range(2):
        for h in range(H):
            s = slot(l, h)
            down, along = cum_t[:, s : s + 1], cum[s : s + 1, :]
            r.DM[l, h] = jnp.exp(jnp.where(causal, down - along, -1e30)).astype(BF)
            r.DTM[l, h] = jnp.exp(jnp.where(anti, along - down, -1e30)).astype(BF)

    arrived(r.SPR, r.s_sp.at[0])

    def take_span(p, total):
        tile = r.SPR[p]
        r.EA[0, p] = jnp.broadcast_to(jnp.exp(tile[0:1, :]), (ar, lw))
        r.EA[1, p] = jnp.broadcast_to(jnp.exp(tile[4:5, :]), (ar, lw))
        return total + tile

    r.ZS[...] = lax.fori_loop(0, np_, take_span, jnp.zeros((8, lw), F32))
    pltpu.make_async_copy(r.ZS, r.ZR.at[z], r.s_sp.at[1]).start()

    def send_zspan(k):
        other = (z + k) % nz
        remote(r.ZS, r.ZR.at[z], r.s_sp_tx.at[1], r.s_sp.at[1], (other * ny + y, f)).start()

    lax.fori_loop(1, nz, lambda k, c: (send_zspan(k), c)[1], 0)

    arrived(r.K1, r.s_small.at[0])
    arrived(r.K2, r.s_small.at[1])
    r.WST[...] = r.K2[:, :D].astype(BF)
    bias_t = jnp.transpose(r.K2[:, D:])
    r.BIAS[...] = bias_t[:8, :]
    arrived(r.ZR, r.s_sp.at[1])

    def take_zspan(p):
        tile = r.ZR[p]
        r.EZ[0, p] = jnp.broadcast_to(jnp.exp(tile[0:1, :]), (ar, lw))
        r.EZ[1, p] = jnp.broadcast_to(jnp.exp(tile[4:5, :]), (ar, lw))

    loop(nz, take_zspan)

    def chain_send(s):
        pltpu.make_async_copy(r.CL.at[s, rows_of(me), lanes_of(me)], r.R1.at[s, me], r.s_a.at[s]).start()

        def one(k, c):
            q = (me + k) % np_
            remote(
                r.CL.at[s, rows_of(q), lanes_of(q)], r.R1.at[s, me], r.s_a_tx.at[s], r.s_a.at[s], plane(q)
            ).start()
            return c

        lax.fori_loop(1, np_, one, 0)

    def chain_planes(s, l, rev):
        arrived(r.R1.at[s], r.s_a.at[s])

        def add(k, t):
            p = np_ - 1 - k if rev else k
            return r.EA[l, p] * t + r.R1[s, p].astype(F32)

        total = lax.fori_loop(0, np_, add, jnp.zeros((ar, lw), F32))
        r.ZT[s] = total.astype(BF)
        pltpu.make_async_copy(r.ZT.at[s], r.RZ.at[s, z], r.s_z.at[s]).start()

        def one(k, c):
            other = (z + k) % nz
            remote(r.ZT.at[s], r.RZ.at[s, z], r.s_z_tx.at[s], r.s_z.at[s], (other * ny + y, f)).start()
            return c

        lax.fori_loop(1, nz, one, 0)

    def chain_return(s, l, rev):
        arrived(r.RZ.at[s], r.s_z.at[s])

        def over(k, o):
            p = nz - 1 - k if rev else k
            new = r.EZ[l, p] * o + r.RZ[s, p].astype(F32)
            return jnp.where((p > z) if rev else (p < z), new, o)

        o = lax.fori_loop(0, nz, over, jnp.zeros((ar, lw), F32))

        def each(k, o):
            p = np_ - 1 - k if rev else k
            r.SB[s, p] = o.astype(BF)
            return r.EA[l, p] * o + r.R1[s, p].astype(F32)

        lax.fori_loop(0, np_, each, o)
        mine = r.OP.at[s, rows_of(me), lanes_of(me)]
        pltpu.make_async_copy(r.SB.at[s, me], mine, r.s_b.at[s]).start()

        def one(k, c):
            q = (me + k) % np_
            remote(r.SB.at[s, q], mine, r.s_b_tx.at[s], r.s_b.at[s], plane(q)).start()
            return c

        lax.fori_loop(1, np_, one, 0)

    seq = blk * nf + f
    nseq = nb * nf
    after, ahead = (seq + 1) % nseq, (seq + nseq - 1) % nseq
    dev_after = (after // nf, after % nf)
    dev_ahead = (ahead // nf, ahead % nf)

    def taps(l, k, j):
        if j is None:
            return conv_shared[l, k : k + 1, :]
        return r.K1[l, k : k + 1, j]

    def quarter(j):
        return pl.ds(pl.multiple_of(j * 256, 256), 256)

    def eighth(j):
        return pl.ds(pl.multiple_of(j * 128, 128), 128)

    tail = pl.ds(HP, 2 * N)
    left = iota((T, 128), 1) < HEAD

    def stacked(v):
        return jnp.concatenate([jnp.where(left, v, 0.0), jnp.where(left, 0.0, v)], axis=0).astype(BF)

    def forward(l, cur):
        r.CUR[l] = cur
        scale = lax.rsqrt(jnp.mean(cur * cur, axis=-1, keepdims=True) + EPS)
        r.HID[...] = (cur * scale * in_gain[l : l + 1, :]).astype(BF)
        weights_wait(l, (0, 1))
        r.BEF[l, 8:, tail] = mm(r.HID[...], r.Ws[l]).astype(BF).astype(F32)

        def values(j):
            at = quarter(j)
            r.BEF[l, 8:, at] = mm(r.HID[...], r.Wv[l, :, at]).astype(BF).astype(F32)

        loop(4, values)
        rim = r.BEF.at[l, pl.ds(0, 8), :]
        remote(r.BEF.at[l, pl.ds(T, 8), :], rim, r.s_rim_tx.at[l], r.s_rim.at[l], dev_after).start()
        weights_wait(l, (2,))

        def gates(j):
            at = quarter(j)
            g = mm(r.HID[...], r.Wg[l, :, at]).astype(BF).astype(F32)
            sig = sigmoid(g)
            r.SG[:, at] = g * sig
            r.DSG[:, at] = sig * (1.0 + g * (1.0 - sig))

        loop(4, gates)
        pre = mmt(r.HID[...], r.WST[...]) + r.BIAS[0:1, :]
        r.SGM[l] = sigmoid(pre)
        step = jnp.maximum(pre, 0.0) + jnp.log1p(jnp.exp(-jnp.abs(pre)))
        hi = step.astype(BF)
        lo = (step - hi.astype(F32)).astype(BF)

        def steps(j):
            at = quarter(j)
            e = r.E[l, :, at]
            r.ST[l, :, at] = mm(hi, e) + mm(lo, e)

        loop(4, steps)
        arrived(rim, r.s_rim.at[l])

        @pl.when(seq == 0)
        def _():
            r.BEF[l, 0:8, :] = jnp.zeros((8, AC), F32)

        def conv(at, j):
            total = taps(l, 0, j) * r.BEF[l, 5 : 5 + T, at]
            for k in range(1, 4):
                total = total + taps(l, k, j) * r.BEF[l, 5 + k : 5 + k + T, at]
            sig = sigmoid(total)
            act = (total * sig).astype(BF)
            r.ACT[l, :, at] = act
            r.DSIL[l, :, at] = sig * (1.0 + total * (1.0 - sig))
            return act.astype(F32)

        bc = conv(tail, None)
        b_t = jnp.transpose(bc[:, :N]).astype(BF)
        r.BT[...] = b_t
        r.CT[l] = jnp.transpose(bc[:, N:]).astype(BF)
        b, c = bc[:, :N].astype(BF), bc[:, N:].astype(BF)
        r.SS[...] = mmt(c, b)
        r.STT[l] = mmt(b, c)

        def inputs(j):
            at = quarter(j)
            act = conv(at, at)
            xs = act * r.ST[l, :, at]
            wx = (xs * r.RM[l, :, at]).astype(BF)
            r.XS[l, :, at] = xs.astype(BF)
            r.WX[l, :, at] = wx
            r.CL[l, :, at] = mm(r.BT[...], wx).astype(BF)

        loop(4, inputs)
        chain_send(l)

        def within(j):
            at = eighth(j)
            scores = r.SS[...]
            m = jnp.concatenate(
                [(r.DM[l, 2 * j].astype(F32) * scores).astype(BF), (r.DM[l, 2 * j + 1].astype(F32) * scores).astype(BF)],
                axis=1,
            )
            skip = r.K1[l, 5:6, at]
            r.Y[:, at] = mm(m, stacked(r.XS[l, :, at].astype(F32))) + skip * r.ACT[l, :, at].astype(F32)

        loop(4, within)
        chain_planes(l, l, False)
        lax.fori_loop(4, 8, lambda j, c: (within(j), c)[1], 0)
        weights_forward_later(l)
        chain_return(l, l, False)
        weights_wait(l, (3,))
        arrived(r.OP.at[l], r.s_b.at[l])

        def finish(j):
            at = quarter(j)
            yy = r.Y[:, at] + r.EC[l, :, at] * mm(r.ACT[l, :, pl.ds(HP + N, N)], r.OP[l, :, at])
            gated = yy * r.SG[:, at]
            rr = lax.rsqrt(mm((gated * gated).astype(BF), r.J[...]) + EPS)
            gn = gated * rr
            r.GN[l, :, at] = gn
            r.HO[:, at] = (gn * r.K1[l, 4:5, at]).astype(BF)
            r.RSG[l, :, at] = rr * r.SG[:, at]
            r.RYD[l, :, at] = rr * yy * r.DSG[:, at]

        loop(4, finish)
        return (r.CUR[l] + mm(r.HO[...], r.Wo[l])).astype(BF)

    def weights_forward_later(l):
        if l == 0:
            weights_forward(1, (0, 1, 2, 3))

    def backward(l):
        s = 3 - l
        u = r.U[...].astype(BF)
        c_t = r.CT[l]

        def enter(j):
            at = quarter(j)
            dn = mmt(u, r.Wo[l, at, :]) * r.K1[l, 4:5, at]
            gn = r.GN[l, :, at]
            t = dn - gn * mm((dn * gn).astype(BF), r.J[...])
            dy = t * r.RSG[l, :, at]
            r.DY[:, at] = dy
            r.DGA[:, at] = (t * r.RYD[l, :, at]).astype(BF)
            q = (r.EC[l, :, at] * dy).astype(BF)
            r.Q[:, at] = q
            r.CL[s, :, at] = mm(c_t, q).astype(BF)

        loop(4, enter)
        chain_send(s)
        r.DS[...] = jnp.zeros((T, T), F32)

        def within(j):
            at = eighth(j)
            dy2 = stacked(r.DY[:, at])
            dm = mmt(dy2, r.XS[l, :, at])
            r.DS[...] += r.DM[l, 2 * j].astype(F32) * dm[:T] + r.DM[l, 2 * j + 1].astype(F32) * dm[T:]
            turned = r.STT[l]
            m_t = jnp.concatenate(
                [(r.DTM[l, 2 * j].astype(F32) * turned).astype(BF), (r.DTM[l, 2 * j + 1].astype(F32) * turned).astype(BF)],
                axis=1,
            )
            r.DXS[:, at] = mm(m_t, dy2)

        loop(4, within)
        chain_planes(s, l, True)
        lax.fori_loop(4, 8, lambda j, c: (within(j), c)[1], 0)
        b, c = r.ACT[l, :, pl.ds(HP, N)], r.ACT[l, :, pl.ds(HP + N, N)]
        ds = r.DS[...]
        r.DBC[:, N:] = mm(ds.astype(BF), b) + mmt(r.Q[...], r.OP[l])
        r.DBC[:, :N] = mm(jnp.transpose(ds).astype(BF), c)
        chain_return(s, l, True)
        r.DH[...] = mmt(r.DGA[...], r.Wg[l])
        arrived(r.OP.at[s], r.s_b.at[s])
        r.DBC[:, :N] += mmt(r.WX[l], r.OP[s])
        r.DTOT[l, 0:T, tail] = r.DBC[...].astype(BF).astype(F32) * r.DSIL[l, :, tail]
        r.DST[...] = jnp.zeros((T, slots), F32)

        def leave(j):
            at = quarter(j)
            b = r.ACT[l, :, pl.ds(HP, N)]
            dxs = r.DXS[:, at] + r.RM[l, :, at] * mm(b, r.OP[s, :, at])
            act = r.ACT[l, :, at].astype(F32)
            dx = dxs * r.ST[l, :, at] + r.K1[l, 5:6, at] * r.DY[:, at]
            r.DST[...] += mm((dxs * act).astype(BF), r.ET[l, at, :])
            r.DTOT[l, 0:T, at] = dx.astype(BF).astype(F32) * r.DSIL[l, :, at]

        loop(4, leave)
        rim = r.DTOT.at[l, pl.ds(T, 8), :]
        remote(r.DTOT.at[l, pl.ds(0, 8), :], rim, r.s_rim_tx.at[s], r.s_rim.at[s], dev_ahead).start()
        r.DH[...] += mm((r.DST[...] * r.SGM[l]).astype(BF), r.WST[...])
        arrived(rim, r.s_rim.at[s])

        @pl.when(seq == nseq - 1)
        def _():
            r.DTOT[l, T:, :] = jnp.zeros((8, AC), F32)

        def unconv(at, j):
            total = taps(l, 0, j) * r.DTOT[l, 3 : 3 + T, at]
            for k in range(1, 4):
                total = total + taps(l, k, j) * r.DTOT[l, 3 - k : 3 - k + T, at]
            r.DB[:, at] = total.astype(BF)

        unconv(tail, None)
        loop(4, lambda j: unconv(quarter(j), quarter(j)))
        dn = r.DH[...] + mmt(r.DB[:, :HP], r.Wv[l]) + mmt(r.DB[:, HP:], r.Ws[l])
        cur = r.CUR[l]
        scale = lax.rsqrt(jnp.mean(cur * cur, axis=-1, keepdims=True) + EPS)
        dg = dn * in_gain[l : l + 1, :]
        dcur = scale * dg - cur * (scale * scale * scale * jnp.mean(cur * dg, axis=-1, keepdims=True))
        return (r.U[...] + dcur).astype(BF)

    def publish(i, staged, out):
        pltpu.make_async_copy(staged, out.at[own, :], r.s_out.at[i]).start()

        def one(k, c):
            g = (f + k) % nf
            remote(staged, out.at[own, :], r.s_out_tx.at[i], r.s_out.at[i], (blk, g)).start()
            return c

        lax.fori_loop(1, nf, one, 0)

    weights_forward(0, (0, 1))
    weights_forward(0, (2, 3))
    weights_send(1, (0, 1, 2, 3))
    in_tok.wait()
    stream = forward(0, r.TOK[...].astype(F32))
    stream = forward(1, stream.astype(F32))
    r.MIXS[...] = stream
    publish(0, r.MIXS, mixed_o)
    in_cot.wait()
    r.U[...] = r.COT[...].astype(F32)
    r.U[...] = backward(1).astype(F32)
    r.GRS[...] = backward(0)
    publish(1, r.GRS, grad_o)

    some = pl.ds(0, (nf - 1) * R2)
    arrived(r.K1.at[:, :, pl.ds(0, (nf - 1) * cw)], r.s_small_tx.at[0])
    arrived(r.K2.at[some, :], r.s_small_tx.at[1])
    arrived(r.LR.at[some, :], r.s_small_tx.at[2])
    for l in range(2):
        for a in range(4):
            arrived(weight_dst(l, a, 0, nf - 1), r.s_w_tx.at[l, a])
    arrived(r.SPR.at[pl.ds(0, np_ - 1)], r.s_sp_tx.at[0])
    arrived(r.ZR.at[pl.ds(0, nz - 1)], r.s_sp_tx.at[1])
    for s in range(4):
        arrived(r.R1.at[s, pl.ds(0, np_ - 1)], r.s_a_tx.at[s])
        arrived(r.RZ.at[s, pl.ds(0, nz - 1)], r.s_z_tx.at[s])
        arrived(r.SB.at[s, pl.ds(0, np_ - 1)], r.s_b_tx.at[s])
        arrived(r.BEF.at[0, pl.ds(0, 8), :], r.s_rim_tx.at[s])
    for i, out in enumerate((mixed_o, grad_o)):
        arrived(out.at[pl.ds(0, (nf - 1) * T), :], r.s_out_tx.at[i])
        arrived(out, r.s_out.at[i])


def body(nb, nf, *args):
    (tokens, cotangent, in_gain, w_pair, w_shared, w_step, step_bias, conv_values, conv_shared, log_decay,
     skip_gain, out_gain, w_out) = args
    hf = H // nf
    lanes = hf * HEAD

    def rep(v):
        return jnp.repeat(v, HEAD, axis=1)[:, None, :]

    pack1 = jnp.concatenate(
        [conv_values, out_gain[:, None, :], rep(skip_gain), jnp.zeros((2, 2, lanes), F32)], axis=1
    )
    steps = jnp.transpose(w_step.astype(F32), (0, 2, 1)).reshape(2 * hf, D)
    bias = jnp.broadcast_to(step_bias.reshape(2 * hf, 1), (2 * hf, 128))
    pack2 = jnp.pad(jnp.concatenate([steps, bias], axis=1), ((0, R2 - 2 * hf), (0, 0)))
    lrp = jnp.transpose(log_decay.reshape(2 * hf, nf, T), (1, 0, 2))
    lrp = jnp.pad(lrp, ((0, 0), (0, R2 - 2 * hf), (0, 0)))
    parts = layout(nb, nf)
    vmem, hbm = pl.BlockSpec(memory_space=pltpu.VMEM), pl.BlockSpec(memory_space=pl.ANY)
    shape = jax.ShapeDtypeStruct(tokens.shape, BF)
    return pl.pallas_call(
        functools.partial(kernel, nb, nf, tuple(parts)),
        out_shape=(shape, shape),
        in_specs=[hbm, hbm, vmem, hbm, hbm, hbm, hbm, hbm, hbm, vmem],
        out_specs=(hbm, hbm),
        scratch_shapes=list(parts.values()),
        compiler_params=pltpu.CompilerParams(has_side_effects=True, vmem_limit_bytes=56 * 2**20),
        name="layers",
    )(tokens, cotangent, in_gain, w_pair, w_shared, w_out, pack1, pack2, lrp, conv_shared)


def solution(mesh):
    nb, nf = mesh.shape["blk"], mesh.shape["fsdp"]
    in_specs = (
        P("blk", None),
        P("blk", None),
        P(),
        P(None, None, None, "fsdp"),
        P(None, "fsdp", None),
        P(None, None, "fsdp"),
        P(None, "fsdp"),
        P(None, None, "fsdp"),
        P(),
        P(None, "fsdp", "blk"),
        P(None, "fsdp"),
        P(None, "fsdp"),
        P(None, "fsdp", None),
    )
    out_specs = (P("blk", None), P("blk", None))
    return jax.shard_map(
        functools.partial(body, nb, nf), mesh=mesh, in_specs=in_specs, out_specs=out_specs, check_vma=False
    )
```

```python
import functools

import jax
import jax.numpy as jnp
from jax import lax
from jax.experimental import pallas as pl
from jax.experimental.pallas import tpu as pltpu
from jax.sharding import PartitionSpec as P

D = 512
H = 16
HEAD = 64
N = 128
T = 128
HP = H * HEAD
AC = HP + 2 * N
EPS = 1e-5
PY = 4
R2 = 8
F32, BF = jnp.float32, jnp.bfloat16
MESH = pl.DeviceIdType.MESH


def mm(a, b):
    return jnp.dot(a, b, preferred_element_type=F32)


def mmt(a, b):
    return lax.dot_general(a, b, (((1,), (1,)), ((), ())), preferred_element_type=F32)


def sigmoid(v):
    return 1.0 / (1.0 + jnp.exp(-v))


def iota(shape, dim):
    return lax.broadcasted_iota(jnp.int32, shape, dim)


def loop(count, fn):
    def step(i, carry):
        fn(i)
        return carry

    lax.fori_loop(0, count, step, 0)


def layout(nb, nf):
    ny, nz = PY, nb // PY
    np_ = ny * nf
    ar, lw = N // nf, HP // ny
    slots = nf * R2
    vm = pltpu.VMEM
    dma = pltpu.SemaphoreType.DMA
    return dict(
        Wv=vm((2, D, HP), BF), Wg=vm((2, D, HP), BF), Wo=vm((2, HP, D), BF), Ws=vm((2, D, 2 * N), BF),
        K1=vm((2, 8, HP), F32), K2=vm((slots, D + 128), F32), LR=vm((slots, T), F32),
        WST=vm((slots, D), BF), BIAS=vm((8, slots), F32), E=vm((2, slots, HP), BF), ET=vm((2, HP, slots), BF),
        J=vm((256, 256), BF), EC=vm((2, T, HP), F32), RM=vm((2, T, HP), F32),
        DM=vm((2, H, T, T), BF), DTM=vm((2, H, T, T), BF),
        SPS=vm((8, HP), F32), SPR=vm((np_, 8, lw), F32), EA=vm((2, np_, ar, lw), F32),
        ZS=vm((8, lw), F32), ZR=vm((nz, 8, lw), F32), EZ=vm((2, nz, ar, lw), F32),
        TOK=vm((T, D), BF), COT=vm((T, D), BF), MIXS=vm((T, D), BF), GRS=vm((T, D), BF),
        CUR=vm((2, T, D), F32), HID=vm((T, D), BF), BEF=vm((2, T + 8, AC), F32), DSIL=vm((2, T, AC), F32),
        ACT=vm((2, T, AC), BF), ST=vm((2, T, HP), F32), SGM=vm((2, T, slots), F32),
        XS=vm((2, T, HP), BF), WX=vm((2, T, HP), BF), BT=vm((N, T), BF), CT=vm((2, N, T), BF),
        SS=vm((T, T), F32), STT=vm((2, T, T), F32), SG=vm((T, HP), F32), DSG=vm((T, HP), F32), Y=vm((T, HP), F32),
        HO=vm((T, HP), BF), GN=vm((2, T, HP), F32), RSG=vm((2, T, HP), F32), RYD=vm((2, T, HP), F32),
        CL=vm((4, N, HP), BF), R1=vm((4, np_, ar, lw), BF), ZT=vm((4, ar, lw), BF), RZ=vm((4, nz, ar, lw), BF),
        SB=vm((4, np_, ar, lw), BF), OP=vm((4, N, HP), BF),
        DY=vm((T, HP), F32), Q=vm((T, HP), BF), DGA=vm((T, HP), BF), DXS=vm((T, HP), F32), DS=vm((T, T), F32),
        DBC=vm((T, 2 * N), F32), DST=vm((T, slots), F32), DTOT=vm((2, T + 8, AC), F32), DB=vm((T, AC), BF),
        DH=vm((T, D), F32), U=vm((T, D), F32),
        s_in=dma((2,)), s_small=dma((3,)), s_small_tx=dma((3,)), s_w=dma((2, 4, 3)), s_sib=dma((2, 4)), s_wloc=dma((2, 4)),
        s_w_tx=dma((2, 4)), s_sp=dma((2,)), s_sp_tx=dma((2,)), s_rim=dma((4,)), s_rim_tx=dma((4,)),
        s_a=dma((4,)), s_a_tx=dma((4,)), s_z=dma((4,)), s_z_tx=dma((4,)), s_b=dma((4, ny)), s_b_tx=dma((4,)),
        s_out=dma((2, 3)), s_out_sib=dma((2,)), s_out_own=dma((2,)), s_out_tx=dma((2,)),
    )


class Refs:
    pass


def kernel(nb, nf, names, *refs):
    (tokens, cot, in_gain, w_pair, w_shared, w_out, pack1, pack2, lrp, conv_shared, mixed_o, grad_o) = refs[:12]
    r = Refs()
    for name, ref in zip(names, refs[12:]):
        setattr(r, name, ref)
    ny, nz = PY, nb // PY
    np_ = ny * nf
    ar, lw = N // nf, HP // ny
    slots = nf * R2
    hf = H // nf
    hf_bits = hf.bit_length() - 1
    cw = HP // nf
    nx = nf // 2
    blk, f = lax.axis_index("blk"), lax.axis_index("fsdp")
    ny_bits, nf_bits = ny.bit_length() - 1, nf.bit_length() - 1
    z, y = blk >> ny_bits, blk & (ny - 1)
    me = y * nf + f
    x, core = f >> 1, f & 1

    def plane(q):
        return (z * ny + (q >> nf_bits), q & (nf - 1))

    def remote(src, dst, tx, rx, dev):
        return pltpu.make_async_remote_copy(
            src_ref=src, dst_ref=dst, send_sem=tx, recv_sem=rx, device_id=dev, device_id_type=MESH
        )

    def arrived(ref, sem):
        pltpu.make_async_copy(ref, ref, sem).wait()

    def slot(l, h):
        return (h // hf) * R2 + l * hf + h % hf

    seq = blk * nf + f
    nseq = nb * nf
    after, ahead = (seq + 1) & (nseq - 1), (seq + nseq - 1) & (nseq - 1)
    dev_after = (after >> nf_bits, after & (nf - 1))
    dev_ahead = (ahead >> nf_bits, ahead & (nf - 1))

    barrier = pltpu.get_barrier_semaphore()

    def greet(dev):
        pl.semaphore_signal(barrier, inc=1, device_id=dev, device_id_type=MESH)

    lax.fori_loop(1, np_, lambda k, c: (greet(plane((me + k) & (np_ - 1))), c)[1], 0)
    lax.fori_loop(1, nz, lambda k, c: (greet((((z + k) & (nz - 1)) * ny + y, f)), c)[1], 0)

    @pl.when(me == np_ - 1)
    def _():
        greet(dev_after)

    @pl.when(me == 0)
    def _():
        greet(dev_ahead)

    own = pl.ds(pl.multiple_of(f * T, T), T)
    in_tok = pltpu.make_async_copy(tokens.at[own, :], r.TOK, r.s_in.at[0])
    in_cot = pltpu.make_async_copy(cot.at[own, :], r.COT, r.s_in.at[1])
    in_tok.start()
    in_cot.start()

    for l in range(2):
        s_at = iota((slots, HP), 0)
        head = iota((slots, HP), 1) >> 6
        want = (head >> hf_bits) * R2 + l * hf + (head & (hf - 1))
        r.E[l] = jnp.where(s_at == want, 1.0, 0.0).astype(BF)
        s_at = iota((HP, slots), 1)
        head = iota((HP, slots), 0) >> 6
        want = (head >> hf_bits) * R2 + l * hf + (head & (hf - 1))
        r.ET[l] = jnp.where(s_at == want, 1.0, 0.0).astype(BF)
    r.J[...] = jnp.where((iota((256, 256), 0) >> 6) == (iota((256, 256), 1) >> 6), 1.0 / HEAD, 0.0).astype(BF)

    rim_peer = jnp.where(jnp.logical_or(me == 0, me == np_ - 1), 1, 0)
    pl.semaphore_wait(barrier, np_ + nz - 2 + rim_peer)
    cols = pl.ds(pl.multiple_of(f * cw, cw), cw)
    rows8 = pl.ds(pl.multiple_of(f * R2, R2), R2)
    pltpu.make_async_copy(pack1, r.K1.at[:, :, cols], r.s_small.at[0]).start()
    pltpu.make_async_copy(pack2, r.K2.at[rows8, :], r.s_small.at[1]).start()
    pltpu.make_async_copy(lrp.at[f], r.LR.at[rows8, :], r.s_small.at[2]).start()

    def send_small(k):
        g = (f + k) & (nf - 1)
        dev = (blk, g)
        remote(lrp.at[g], r.LR.at[rows8, :], r.s_small_tx.at[2], r.s_small.at[2], dev).start()
        remote(pack1, r.K1.at[:, :, cols], r.s_small_tx.at[0], r.s_small.at[0], dev).start()
        remote(pack2, r.K2.at[rows8, :], r.s_small_tx.at[1], r.s_small.at[1], dev).start()

    lax.fori_loop(1, nf, lambda k, c: (send_small(k), c)[1], 0)

    def weight_src(l, a):
        return [w_shared.at[l], w_pair.at[l, 0], w_pair.at[l, 1], w_out.at[l]][a]

    def weight_dst(l, a, g, count=1):
        if a == 0:
            m = D // nf
            return r.Ws.at[l, pl.ds(pl.multiple_of(g * m, m), m * count), :]
        if a == 3:
            return r.Wo.at[l, pl.ds(pl.multiple_of(g * cw, cw), cw * count), :]
        return (r.Wv if a == 1 else r.Wg).at[l, :, pl.ds(pl.multiple_of(g * cw, cw), cw * count)]

    sibling = (blk, x * 2 + 1 - core)

    way = 1 - 2 * core

    def peer(dx):
        return (blk, ((x + nx + dx) & (nx - 1)) * 2 + core)

    def shard_of(dx):
        return ((x + nx + dx) & (nx - 1)) * 2 + core

    def weights_send(l, arrays):
        for a in arrays:
            mine = weight_dst(l, a, f)
            src, tx = weight_src(l, a), r.s_w_tx.at[l, a]
            pltpu.make_async_copy(src, mine, r.s_wloc.at[l, a]).start()
            remote(src, mine, tx, r.s_w.at[l, a, 0], peer(way)).start()
            remote(src, mine, tx, r.s_w.at[l, a, 1], peer(-way)).start()
            remote(src, mine, tx, r.s_sib.at[l, a], sibling).start()

    def weights_pass(l, a, i, dx, relay):
        part = weight_dst(l, a, shard_of(dx))
        arrived(part, r.s_w.at[l, a, i])
        if relay:
            remote(part, part, r.s_w_tx.at[l, a], r.s_w.at[l, a, 2], peer(way)).start()
        remote(part, part, r.s_w_tx.at[l, a], r.s_sib.at[l, a], sibling).start()

    def weights_relay(l, arrays):
        for a in arrays:
            weights_pass(l, a, 0, -way, True)
            weights_pass(l, a, 1, way, False)

    def weights_last(l, arrays):
        for a in arrays:
            weights_pass(l, a, 2, 2, False)

    def weights_wait(l, arrays):
        for a in arrays:
            pltpu.make_async_copy(weight_src(l, a), weight_dst(l, a, f), r.s_wloc.at[l, a]).wait()
            arrived(weight_dst(l, a, 0, nx), r.s_sib.at[l, a])

    weights_send(0, (0, 1, 2, 3))

    def expand(v, l, at):
        hi = v.astype(BF)
        rest = v - hi.astype(F32)
        mid = rest.astype(BF)
        lo = (rest - mid.astype(F32)).astype(BF)
        e = r.E[l, :, at]
        return mm(hi, e) + mm(mid, e) + mm(lo, e)

    arrived(r.LR, r.s_small.at[2])
    upper = jnp.where(iota((T, T), 0) <= iota((T, T), 1), 1.0, 0.0)
    cum = jnp.dot(r.LR[...], upper, preferred_element_type=F32, precision=lax.Precision.HIGHEST)
    cum_t = jnp.transpose(cum)
    spans = [expand(cum_t[T - 8 :, :], l, slice(None))[7:8, :] for l in range(2)]
    r.SPS[...] = jnp.where(iota((8, HP), 0) < 4, spans[0], spans[1])

    def lanes_of(q):
        return pl.ds(pl.multiple_of((q >> nf_bits) * lw, lw), lw)

    def rows_of(q):
        return pl.ds(pl.multiple_of((q & (nf - 1)) * ar, ar), ar)

    pltpu.make_async_copy(r.SPS.at[:, lanes_of(me)], r.SPR.at[me], r.s_sp.at[0]).start()

    def send_span(k):
        q = (me + k) & (np_ - 1)
        remote(r.SPS.at[:, lanes_of(q)], r.SPR.at[me], r.s_sp_tx.at[0], r.s_sp.at[0], plane(q)).start()

    lax.fori_loop(1, np_, lambda k, c: (send_span(k), c)[1], 0)

    ecum = jnp.exp(cum_t)
    remain = jnp.exp(cum_t[T - 1 :, :] - cum_t)
    for l in range(2):
        for j in range(4):
            at = pl.ds(j * 256, 256)
            r.EC[l, :, at] = expand(ecum, l, at)
            r.RM[l, :, at] = expand(remain, l, at)
    causal = iota((T, T), 0) >= iota((T, T), 1)
    anti = iota((T, T), 0) <= iota((T, T), 1)
    for l in range(2):
        for h in range(H):
            s = slot(l, h)
            down, along = cum_t[:, s : s + 1], cum[s : s + 1, :]
            r.DM[l, h] = jnp.exp(jnp.where(causal, down - along, -1e30)).astype(BF)
            r.DTM[l, h] = jnp.exp(jnp.where(anti, along - down, -1e30)).astype(BF)

    arrived(r.K1, r.s_small.at[0])
    arrived(r.K2, r.s_small.at[1])
    r.WST[...] = r.K2[:, :D].astype(BF)
    bias_t = jnp.transpose(r.K2[:, D:])
    r.BIAS[...] = bias_t[:8, :]
    def plane_spans():
        arrived(r.SPR, r.s_sp.at[0])

        def take_span(p, total):
            tile = r.SPR[p]
            r.EA[0, p] = jnp.broadcast_to(jnp.exp(tile[0:1, :]), (ar, lw))
            r.EA[1, p] = jnp.broadcast_to(jnp.exp(tile[4:5, :]), (ar, lw))
            return total + tile

        r.ZS[...] = lax.fori_loop(0, np_, take_span, jnp.zeros((8, lw), F32))
        pltpu.make_async_copy(r.ZS, r.ZR.at[z], r.s_sp.at[1]).start()

        def send_zspan(k):
            other = (z + k) & (nz - 1)
            remote(r.ZS, r.ZR.at[z], r.s_sp_tx.at[1], r.s_sp.at[1], (other * ny + y, f)).start()

        lax.fori_loop(1, nz, lambda k, c: (send_zspan(k), c)[1], 0)

    def world_spans():
        arrived(r.ZR, r.s_sp.at[1])

        def take_zspan(p):
            tile = r.ZR[p]
            r.EZ[0, p] = jnp.broadcast_to(jnp.exp(tile[0:1, :]), (ar, lw))
            r.EZ[1, p] = jnp.broadcast_to(jnp.exp(tile[4:5, :]), (ar, lw))

        loop(nz, take_zspan)

    def chain_send(s, yy, first):
        def one(k, c):
            g = (f + k) & (nf - 1)
            rows = pl.ds(pl.multiple_of(g * ar, ar), ar)
            at = pl.ds(pl.multiple_of(yy * lw, lw), lw)
            remote(
                r.CL.at[s, rows, at], r.R1.at[s, me], r.s_a_tx.at[s], r.s_a.at[s], (z * ny + yy, g)
            ).start()
            return c

        lax.fori_loop(first, nf, one, 0)

    def chain_quarters(s, make):
        def one(j, c):
            yy = (y + j) & (ny - 1)
            make(yy)
            chain_send(s, yy, 0)
            return c

        lax.fori_loop(1, ny, one, 0)
        make(y)
        pltpu.make_async_copy(r.CL.at[s, rows_of(me), lanes_of(me)], r.R1.at[s, me], r.s_a.at[s]).start()
        chain_send(s, y, 1)

    def chain_take(s, use):
        def one(j, c):
            yy = (y + ny - j) & (ny - 1)
            arrived(r.OP.at[s, :, pl.ds(pl.multiple_of(yy * lw, lw), lw)], r.s_b.at[s, yy])
            use(yy)
            return c

        lax.fori_loop(1, ny + 1, one, 0)

    def chain_planes(s, l, rev):
        arrived(r.R1.at[s], r.s_a.at[s])

        def add(k, t):
            p = np_ - 1 - k if rev else k
            return r.EA[l, p] * t + r.R1[s, p].astype(F32)

        total = lax.fori_loop(0, np_, add, jnp.zeros((ar, lw), F32), unroll=8)
        r.ZT[s] = total.astype(BF)
        pltpu.make_async_copy(r.ZT.at[s], r.RZ.at[s, z], r.s_z.at[s]).start()

        def one(k, c):
            other = (z + k) & (nz - 1)
            remote(r.ZT.at[s], r.RZ.at[s, z], r.s_z_tx.at[s], r.s_z.at[s], (other * ny + y, f)).start()
            return c

        lax.fori_loop(1, nz, one, 0)

    def chain_return(s, l, rev):
        arrived(r.RZ.at[s], r.s_z.at[s])

        def over(k, o):
            p = nz - 1 - k if rev else k
            new = r.EZ[l, p] * o + r.RZ[s, p].astype(F32)
            return jnp.where((p > z) if rev else (p < z), new, o)

        o = lax.fori_loop(0, nz, over, jnp.zeros((ar, lw), F32), unroll=True)

        def each(k, o):
            p = np_ - 1 - k if rev else k
            r.SB[s, p] = o.astype(BF)
            return r.EA[l, p] * o + r.R1[s, p].astype(F32)

        lax.fori_loop(0, np_, each, o, unroll=8)
        mine = r.OP.at[s, rows_of(me), lanes_of(me)]
        pltpu.make_async_copy(r.SB.at[s, me], mine, r.s_b.at[s, y]).start()

        def one(k, c):
            q = (me + k) & (np_ - 1)
            remote(r.SB.at[s, q], mine, r.s_b_tx.at[s], r.s_b.at[s, y], plane(q)).start()
            return c

        lax.fori_loop(1, np_, one, 0)

    def taps(l, k, j):
        if j is None:
            return conv_shared[l, k : k + 1, :]
        return r.K1[l, k : k + 1, j]

    def quarter(j):
        return pl.ds(pl.multiple_of(j * 256, 256), 256)

    def eighth(j):
        return pl.ds(pl.multiple_of(j * 128, 128), 128)

    tail = pl.ds(HP, 2 * N)
    left = iota((T, 128), 1) < HEAD

    def stacked(v):
        return jnp.concatenate([jnp.where(left, v, 0.0), jnp.where(left, 0.0, v)], axis=0).astype(BF)

    def forward(l, cur):
        r.CUR[l] = cur
        scale = lax.rsqrt(jnp.mean(cur * cur, axis=-1, keepdims=True) + EPS)
        r.HID[...] = (cur * scale * in_gain[l : l + 1, :]).astype(BF)
        weights_wait(l, (0, 1))
        r.BEF[l, 8:, tail] = mm(r.HID[...], r.Ws[l]).astype(BF).astype(F32)

        def values(j):
            at = quarter(j)
            r.BEF[l, 8:, at] = mm(r.HID[...], r.Wv[l, :, at]).astype(BF).astype(F32)

        loop(4, values)
        rim = r.BEF.at[l, pl.ds(0, 8), :]
        remote(r.BEF.at[l, pl.ds(T, 8), :], rim, r.s_rim_tx.at[l], r.s_rim.at[l], dev_after).start()
        if l == 0:
            weights_relay(0, (2, 3))
            weights_last(0, (2,))
            weights_send(1, (0, 1, 2, 3))
        weights_wait(l, (2,))

        def gates(j):
            at = quarter(j)
            g = mm(r.HID[...], r.Wg[l, :, at]).astype(BF).astype(F32)
            sig = sigmoid(g)
            r.SG[:, at] = g * sig
            r.DSG[:, at] = sig * (1.0 + g * (1.0 - sig))

        loop(4, gates)
        pre = mmt(r.HID[...], r.WST[...]) + r.BIAS[0:1, :]
        r.SGM[l] = sigmoid(pre)
        step = jnp.maximum(pre, 0.0) + jnp.log1p(jnp.exp(-jnp.abs(pre)))
        hi = step.astype(BF)
        lo = (step - hi.astype(F32)).astype(BF)

        def steps(j):
            at = quarter(j)
            e = r.E[l, :, at]
            r.ST[l, :, at] = mm(hi, e) + mm(lo, e)

        loop(4, steps)
        arrived(rim, r.s_rim.at[l])

        @pl.when(seq == 0)
        def _():
            r.BEF[l, 0:8, :] = jnp.zeros((8, AC), F32)

        def conv(at, j):
            total = taps(l, 0, j) * r.BEF[l, 5 : 5 + T, at]
            for k in range(1, 4):
                total = total + taps(l, k, j) * r.BEF[l, 5 + k : 5 + k + T, at]
            sig = sigmoid(total)
            act = (total * sig).astype(BF)
            r.ACT[l, :, at] = act
            r.DSIL[l, :, at] = sig * (1.0 + total * (1.0 - sig))
            return act.astype(F32)

        bc = conv(tail, None)
        b_t = jnp.transpose(bc[:, :N]).astype(BF)
        r.BT[...] = b_t
        r.CT[l] = jnp.transpose(bc[:, N:]).astype(BF)
        b, c = bc[:, :N].astype(BF), bc[:, N:].astype(BF)
        r.SS[...] = mmt(c, b)
        r.STT[l] = mmt(b, c)

        def inputs(j):
            at = quarter(j)
            act = conv(at, at)
            xs = act * r.ST[l, :, at]
            wx = (xs * r.RM[l, :, at]).astype(BF)
            r.XS[l, :, at] = xs.astype(BF)
            r.WX[l, :, at] = wx
            r.CL[l, :, at] = mm(r.BT[...], wx).astype(BF)

        chain_quarters(l, inputs)
        if l == 0:
            weights_last(0, (3,))
            plane_spans()

        def within(j):
            at = eighth(j)
            scores = r.SS[...]
            m = jnp.concatenate(
                [(r.DM[l, 2 * j].astype(F32) * scores).astype(BF), (r.DM[l, 2 * j + 1].astype(F32) * scores).astype(BF)],
                axis=1,
            )
            skip = r.K1[l, 5:6, at]
            r.Y[:, at] = mm(m, stacked(r.XS[l, :, at].astype(F32))) + skip * r.ACT[l, :, at].astype(F32)

        loop(4, within)
        chain_planes(l, l, False)
        lax.fori_loop(4, 8, lambda j, c: (within(j), c)[1], 0)
        if l == 0:
            weights_relay(1, (0, 1, 2, 3))
            world_spans()
        chain_return(l, l, False)
        if l == 0:
            weights_last(1, (0, 1, 2, 3))
        weights_wait(l, (3,))

        def finish(j):
            at = quarter(j)
            yy = r.Y[:, at] + r.EC[l, :, at] * mm(r.ACT[l, :, pl.ds(HP + N, N)], r.OP[l, :, at])
            gated = yy * r.SG[:, at]
            rr = lax.rsqrt(mm((gated * gated).astype(BF), r.J[...]) + EPS)
            gn = gated * rr
            r.GN[l, :, at] = gn
            r.HO[:, at] = (gn * r.K1[l, 4:5, at]).astype(BF)
            r.RSG[l, :, at] = rr * r.SG[:, at]
            r.RYD[l, :, at] = rr * yy * r.DSG[:, at]

        chain_take(l, finish)
        return (r.CUR[l] + mm(r.HO[...], r.Wo[l])).astype(BF)

    def backward(l):
        s = 3 - l
        u = r.U[...].astype(BF)
        c_t = r.CT[l]

        def enter(j):
            at = quarter(j)
            dn = mmt(u, r.Wo[l, at, :]) * r.K1[l, 4:5, at]
            gn = r.GN[l, :, at]
            t = dn - gn * mm((dn * gn).astype(BF), r.J[...])
            dy = t * r.RSG[l, :, at]
            r.DY[:, at] = dy
            r.DGA[:, at] = (t * r.RYD[l, :, at]).astype(BF)
            q = (r.EC[l, :, at] * dy).astype(BF)
            r.Q[:, at] = q
            r.CL[s, :, at] = mm(c_t, q).astype(BF)

        chain_quarters(s, enter)
        r.DS[...] = jnp.zeros((T, T), F32)

        def within(j):
            at = eighth(j)
            dy2 = stacked(r.DY[:, at])
            dm = mmt(dy2, r.XS[l, :, at])
            r.DS[...] += r.DM[l, 2 * j].astype(F32) * dm[:T] + r.DM[l, 2 * j + 1].astype(F32) * dm[T:]
            turned = r.STT[l]
            m_t = jnp.concatenate(
                [(r.DTM[l, 2 * j].astype(F32) * turned).astype(BF), (r.DTM[l, 2 * j + 1].astype(F32) * turned).astype(BF)],
                axis=1,
            )
            r.DXS[:, at] = mm(m_t, dy2)

        loop(4, within)
        chain_planes(s, l, True)
        if l == 1:
            publish_relay(0, mixed_o)
        lax.fori_loop(4, 8, lambda j, c: (within(j), c)[1], 0)
        b, c = r.ACT[l, :, pl.ds(HP, N)], r.ACT[l, :, pl.ds(HP + N, N)]
        ds = r.DS[...]
        r.DBC[:, N:] = mm(ds.astype(BF), b) + mmt(r.Q[...], r.OP[l])
        r.DBC[:, :N] = mm(jnp.transpose(ds).astype(BF), c)
        chain_return(s, l, True)
        if l == 1:
            publish_last(0, mixed_o)
        r.DST[...] = jnp.zeros((T, slots), F32)

        def leave(j):
            at = quarter(j)
            b = r.ACT[l, :, pl.ds(HP, N)]
            g = r.OP[s, :, at]
            r.DBC[:, :N] += mmt(r.WX[l, :, at], g)
            dxs = r.DXS[:, at] + r.RM[l, :, at] * mm(b, g)
            act = r.ACT[l, :, at].astype(F32)
            dx = dxs * r.ST[l, :, at] + r.K1[l, 5:6, at] * r.DY[:, at]
            r.DST[...] += mm((dxs * act).astype(BF), r.ET[l, at, :])
            r.DTOT[l, 0:T, at] = dx.astype(BF).astype(F32) * r.DSIL[l, :, at]

        chain_take(s, leave)
        r.DTOT[l, 0:T, tail] = r.DBC[...].astype(BF).astype(F32) * r.DSIL[l, :, tail]
        rim = r.DTOT.at[l, pl.ds(T, 8), :]
        remote(r.DTOT.at[l, pl.ds(0, 8), :], rim, r.s_rim_tx.at[s], r.s_rim.at[s], dev_ahead).start()
        r.DH[...] = mmt(r.DGA[...], r.Wg[l]) + mm((r.DST[...] * r.SGM[l]).astype(BF), r.WST[...])
        arrived(rim, r.s_rim.at[s])

        @pl.when(seq == nseq - 1)
        def _():
            r.DTOT[l, T:, :] = jnp.zeros((8, AC), F32)

        def unconv(at, j):
            total = taps(l, 0, j) * r.DTOT[l, 3 : 3 + T, at]
            for k in range(1, 4):
                total = total + taps(l, k, j) * r.DTOT[l, 3 - k : 3 - k + T, at]
            r.DB[:, at] = total.astype(BF)

        unconv(tail, None)
        loop(4, lambda j: unconv(quarter(j), quarter(j)))
        dn = r.DH[...] + mmt(r.DB[:, :HP], r.Wv[l]) + mmt(r.DB[:, HP:], r.Ws[l])
        cur = r.CUR[l]
        scale = lax.rsqrt(jnp.mean(cur * cur, axis=-1, keepdims=True) + EPS)
        dg = dn * in_gain[l : l + 1, :]
        dcur = scale * dg - cur * (scale * scale * scale * jnp.mean(cur * dg, axis=-1, keepdims=True))
        return (r.U[...] + dcur).astype(BF)

    def rows_at(g):
        return pl.ds(pl.multiple_of(g * T, T), T)

    def publish(i, staged, out):
        tx = r.s_out_tx.at[i]
        pltpu.make_async_copy(staged, out.at[own, :], r.s_out_own.at[i]).start()
        remote(staged, out.at[own, :], tx, r.s_out.at[i, 0], peer(way)).start()
        remote(staged, out.at[own, :], tx, r.s_out.at[i, 1], peer(-way)).start()
        remote(staged, out.at[own, :], tx, r.s_out_sib.at[i], sibling).start()

    def publish_pass(i, out, k, dx, relay):
        part = out.at[rows_at(shard_of(dx)), :]
        arrived(part, r.s_out.at[i, k])
        if relay:
            remote(part, part, r.s_out_tx.at[i], r.s_out.at[i, 2], peer(way)).start()
        remote(part, part, r.s_out_tx.at[i], r.s_out_sib.at[i], sibling).start()

    def publish_relay(i, out):
        publish_pass(i, out, 0, -way, True)
        publish_pass(i, out, 1, way, False)

    def publish_last(i, out):
        publish_pass(i, out, 2, 2, False)

    weights_relay(0, (0, 1))
    weights_last(0, (0, 1))
    in_tok.wait()
    stream = forward(0, r.TOK[...].astype(F32))
    stream = forward(1, stream.astype(F32))
    r.MIXS[...] = stream
    publish(0, r.MIXS, mixed_o)
    in_cot.wait()
    r.U[...] = r.COT[...].astype(F32)
    r.U[...] = backward(1).astype(F32)
    r.GRS[...] = backward(0)
    publish(1, r.GRS, grad_o)
    publish_relay(1, grad_o)
    publish_last(1, grad_o)

    some = pl.ds(0, (nf - 1) * R2)
    arrived(r.K1.at[:, :, pl.ds(0, (nf - 1) * cw)], r.s_small_tx.at[0])
    arrived(r.K2.at[some, :], r.s_small_tx.at[1])
    arrived(r.LR.at[some, :], r.s_small_tx.at[2])
    for l in range(2):
        for a in range(4):
            arrived(weight_dst(l, a, 0, nf - 1), r.s_w_tx.at[l, a])
    arrived(r.SPR.at[pl.ds(0, np_ - 1)], r.s_sp_tx.at[0])
    arrived(r.ZR.at[pl.ds(0, nz - 1)], r.s_sp_tx.at[1])
    for s in range(4):
        arrived(r.R1.at[s, pl.ds(0, np_ - 1)], r.s_a_tx.at[s])
        arrived(r.RZ.at[s, pl.ds(0, nz - 1)], r.s_z_tx.at[s])
        arrived(r.SB.at[s, pl.ds(0, np_ - 1)], r.s_b_tx.at[s])
        arrived(r.BEF.at[0, pl.ds(0, 8), :], r.s_rim_tx.at[s])
    for i, out in enumerate((mixed_o, grad_o)):
        arrived(out.at[pl.ds(0, (nf - 1) * T), :], r.s_out_tx.at[i])
        arrived(out.at[pl.ds(0, nx * T), :], r.s_out_sib.at[i])
        arrived(out.at[own, :], r.s_out_own.at[i])


def body(nb, nf, *args):
    (tokens, cotangent, in_gain, w_pair, w_shared, w_step, step_bias, conv_values, conv_shared, log_decay,
     skip_gain, out_gain, w_out) = args
    hf = H // nf
    lanes = hf * HEAD

    def rep(v):
        return jnp.repeat(v, HEAD, axis=1)[:, None, :]

    pack1 = jnp.concatenate(
        [conv_values, out_gain[:, None, :], rep(skip_gain), jnp.zeros((2, 2, lanes), F32)], axis=1
    )
    steps = jnp.transpose(w_step.astype(F32), (0, 2, 1)).reshape(2 * hf, D)
    bias = jnp.broadcast_to(step_bias.reshape(2 * hf, 1), (2 * hf, 128))
    pack2 = jnp.pad(jnp.concatenate([steps, bias], axis=1), ((0, R2 - 2 * hf), (0, 0)))
    lrp = jnp.transpose(log_decay.reshape(2 * hf, nf, T), (1, 0, 2))
    lrp = jnp.pad(lrp, ((0, 0), (0, R2 - 2 * hf), (0, 0)))
    parts = layout(nb, nf)
    vmem, hbm = pl.BlockSpec(memory_space=pltpu.VMEM), pl.BlockSpec(memory_space=pl.ANY)
    shape = jax.ShapeDtypeStruct(tokens.shape, BF)
    return pl.pallas_call(
        functools.partial(kernel, nb, nf, tuple(parts)),
        out_shape=(pltpu.VMEM(tokens.shape, BF), pltpu.VMEM(tokens.shape, BF)),
        in_specs=[hbm, hbm, vmem, hbm, hbm, hbm, hbm, hbm, hbm, vmem],
        out_specs=(hbm, hbm),
        scratch_shapes=list(parts.values()),
        compiler_params=pltpu.CompilerParams(has_side_effects=True, collective_id=0, vmem_limit_bytes=56 * 2**20),
        name="layers",
    )(tokens, cotangent, in_gain, w_pair, w_shared, w_out, pack1, pack2, lrp, conv_shared)


def solution(mesh):
    nb, nf = mesh.shape["blk"], mesh.shape["fsdp"]
    in_specs = (
        P("blk", None),
        P("blk", None),
        P(),
        P(None, None, None, "fsdp"),
        P(None, "fsdp", None),
        P(None, None, "fsdp"),
        P(None, "fsdp"),
        P(None, None, "fsdp"),
        P(),
        P(None, "fsdp", "blk"),
        P(None, "fsdp"),
        P(None, "fsdp"),
        P(None, "fsdp", None),
    )
    out_specs = (P("blk", None), P("blk", None))
    return jax.shard_map(
        functools.partial(body, nb, nf), mesh=mesh, in_specs=in_specs, out_specs=out_specs, check_vma=False
    )
```

```python
import functools

import jax
import jax.numpy as jnp
from jax import lax
from jax.experimental import pallas as pl
from jax.experimental.pallas import tpu as pltpu
from jax.sharding import PartitionSpec as P

D = 512
H = 16
HEAD = 64
N = 128
T = 128
HP = H * HEAD
AC = HP + 2 * N
EPS = 1e-5
PY = 4
R2 = 8
F32, BF = jnp.float32, jnp.bfloat16
MESH = pl.DeviceIdType.MESH


def mm(a, b):
    return jnp.dot(a, b, preferred_element_type=F32)


def mmt(a, b):
    return lax.dot_general(a, b, (((1,), (1,)), ((), ())), preferred_element_type=F32)


def sigmoid(v):
    return 1.0 / (1.0 + jnp.exp(-v))


def iota(shape, dim):
    return lax.broadcasted_iota(jnp.int32, shape, dim)


def loop(count, fn):
    def step(i, carry):
        fn(i)
        return carry

    lax.fori_loop(0, count, step, 0, unroll=True)


def layout(nb, nf):
    ny, nz = PY, nb // PY
    np_ = ny * nf
    ar, lw = N // nf, HP // ny
    slots = nf * R2
    hf = H // nf
    vm = pltpu.VMEM
    dma = pltpu.SemaphoreType.DMA
    return dict(
        Wv=vm((2, D, HP), BF), Wg=vm((2, D, HP), BF), Wo=vm((2, HP, D), BF), Ws=vm((2, D, 2 * N), BF),
        K1=vm((2, 8, HP), F32), K2=vm((slots, D + 128), F32), LR=vm((slots, T), F32),
        WST=vm((slots, D), BF), BIAS=vm((8, slots), F32), E=vm((2, slots, HP), BF), ET=vm((2, HP, slots), BF),
        J=vm((256, 256), BF), EC=vm((2, T, HP), F32), RM=vm((2, T, HP), F32),
        DM=vm((2, H, T, T), BF), DTM=vm((2, H, T, T), BF),
        SPS=vm((8, HP), F32), SPR=vm((np_, 8, lw), F32), EA=vm((2, np_, ar, lw), F32),
        ZS=vm((8, lw), F32), ZR=vm((nz, 8, lw), F32), EZ=vm((2, nz, ar, lw), F32),
        TOK=vm((T, D), BF), COT=vm((T, D), BF), MIXS=vm((T, D), BF), GRS=vm((T, D), BF),
        CUR=vm((2, T, D), F32), HID=vm((T, D), BF), BEF=vm((2, T + 8, AC), F32), DSIL=vm((2, T, AC), F32),
        ACT=vm((2, T, AC), BF), ST=vm((2, T, HP), F32), SGM=vm((2, T, slots), F32),
        XS=vm((2, T, HP), BF), WX=vm((2, T, HP), BF), BT=vm((N, T), BF), CT=vm((2, N, T), BF),
        SS=vm((T, T), F32), STT=vm((2, T, T), F32), SG=vm((T, HP), F32), DSG=vm((T, HP), F32), Y=vm((T, HP), F32),
        HO=vm((T, HP), BF), GN=vm((2, T, HP), F32), RSG=vm((2, T, HP), F32), RYD=vm((2, T, HP), F32),
        CL=vm((4, N, HP), BF), R1=vm((4, np_, ar, lw), BF), ZT=vm((4, ar, lw), BF), RZ=vm((4, nz, ar, lw), BF),
        SB=vm((4, np_, ar, lw), BF), OP=vm((4, N, HP), BF),
        DY=vm((T, HP), F32), Q=vm((T, HP), BF), DGA=vm((T, HP), BF), DXS=vm((T, HP), F32), DS=vm((T, T), F32),
        DBC=vm((T, 2 * N), F32), DST=vm((T, slots), F32), DTOT=vm((2, T + 8, AC), F32), DB=vm((T, AC), BF),
        DH=vm((T, D), F32), U=vm((T, D), F32),
        P1=vm((2, 8, hf * HEAD), F32), P2=vm((R2, D + 128), F32), P3=vm((nf, R2, T), F32), s_in=dma((2,)), s_small=dma((3,)), s_small_tx=dma((3,)), s_w=dma((2, 4, 3)), s_sib=dma((2, 4)), s_wloc=dma((2, 4)),
        s_w_tx=dma((2, 4)), s_sp=dma((2,)), s_sp_tx=dma((2,)), s_rim=dma((4,)), s_rim_tx=dma((4,)),
        s_a=dma((4,)), s_a_tx=dma((4,)), s_z=dma((4,)), s_z_tx=dma((4,)), s_b=dma((4, ny)), s_b_tx=dma((4,)),
        s_out=dma((2, 3)), s_out_sib=dma((2,)), s_out_own=dma((2,)), s_out_tx=dma((2,)),
    )


class Refs:
    pass


def kernel(nb, nf, names, *refs):
    (tokens, cot, in_gain, w_pair, w_shared, w_out, conv_values, out_gain, skip_gain, steps, step_bias, rates,
     conv_shared, mixed_o, grad_o) = refs[:15]
    r = Refs()
    for name, ref in zip(names, refs[15:]):
        setattr(r, name, ref)
    ny, nz = PY, nb // PY
    np_ = ny * nf
    ar, lw = N // nf, HP // ny
    slots = nf * R2
    hf = H // nf
    hf_bits = hf.bit_length() - 1
    cw = HP // nf
    nx = nf // 2
    blk, f = lax.axis_index("blk"), lax.axis_index("fsdp")
    ny_bits, nf_bits = ny.bit_length() - 1, nf.bit_length() - 1
    z, y = blk >> ny_bits, blk & (ny - 1)
    me = y * nf + f
    x, core = f >> 1, f & 1

    def plane(q):
        return (z * ny + (q >> nf_bits), q & (nf - 1))

    def remote(src, dst, tx, rx, dev):
        return pltpu.make_async_remote_copy(
            src_ref=src, dst_ref=dst, send_sem=tx, recv_sem=rx, device_id=dev, device_id_type=MESH
        )

    def arrived(ref, sem):
        pltpu.make_async_copy(ref, ref, sem).wait()

    def slot(l, h):
        return (h // hf) * R2 + l * hf + h % hf

    seq = blk * nf + f
    nseq = nb * nf
    after, ahead = (seq + 1) & (nseq - 1), (seq + nseq - 1) & (nseq - 1)
    dev_after = (after >> nf_bits, after & (nf - 1))
    dev_ahead = (ahead >> nf_bits, ahead & (nf - 1))

    barrier = pltpu.get_barrier_semaphore()

    def greet(dev):
        pl.semaphore_signal(barrier, inc=1, device_id=dev, device_id_type=MESH)

    lax.fori_loop(1, np_, lambda k, c: (greet(plane((me + k) & (np_ - 1))), c)[1], 0)
    lax.fori_loop(1, nz, lambda k, c: (greet((((z + k) & (nz - 1)) * ny + y, f)), c)[1], 0)

    @pl.when(me == np_ - 1)
    def _():
        greet(dev_after)

    @pl.when(me == 0)
    def _():
        greet(dev_ahead)

    own = pl.ds(pl.multiple_of(f * T, T), T)
    in_tok = pltpu.make_async_copy(tokens.at[own, :], r.TOK, r.s_in.at[0])
    in_cot = pltpu.make_async_copy(cot.at[own, :], r.COT, r.s_in.at[1])
    in_tok.start()
    in_cot.start()

    for l in range(2):
        s_at = iota((slots, HP), 0)
        head = iota((slots, HP), 1) >> 6
        want = (head >> hf_bits) * R2 + l * hf + (head & (hf - 1))
        r.E[l] = jnp.where(s_at == want, 1.0, 0.0).astype(BF)
        s_at = iota((HP, slots), 1)
        head = iota((HP, slots), 0) >> 6
        want = (head >> hf_bits) * R2 + l * hf + (head & (hf - 1))
        r.ET[l] = jnp.where(s_at == want, 1.0, 0.0).astype(BF)
    r.J[...] = jnp.where((iota((256, 256), 0) >> 6) == (iota((256, 256), 1) >> 6), 1.0 / HEAD, 0.0).astype(BF)

    pack1, pack2, lrp = r.P1, r.P2, r.P3
    if hf * 2 < R2:
        pack2[...] = jnp.zeros((R2, D + 128), F32)
        lrp[...] = jnp.zeros((nf, R2, T), F32)
    for l in range(2):
        pack1[l, 0:4, :] = conv_values[l]
        pack1[l, 4:5, :] = out_gain[l : l + 1, :]
        for h in range(hf):
            pack1[l, 5:6, h * HEAD : (h + 1) * HEAD] = jnp.broadcast_to(skip_gain[l : l + 1, h : h + 1], (1, HEAD))
            row = l * hf + h
            pack2[row : row + 1, D:] = jnp.broadcast_to(step_bias[l : l + 1, h : h + 1], (1, 128))
            pack2[row : row + 1, :D] = steps[l, h : h + 1, :]
            for g in range(nf):
                lrp[g, row : row + 1, :] = rates[l, h : h + 1, g * T : (g + 1) * T]
        pack1[l, 6:8, :] = jnp.zeros((2, hf * HEAD), F32)
    rim_peer = jnp.where(jnp.logical_or(me == 0, me == np_ - 1), 1, 0)
    pl.semaphore_wait(barrier, np_ + nz - 2 + rim_peer)
    cols = pl.ds(pl.multiple_of(f * cw, cw), cw)
    rows8 = pl.ds(pl.multiple_of(f * R2, R2), R2)
    pltpu.make_async_copy(pack1, r.K1.at[:, :, cols], r.s_small.at[0]).start()
    pltpu.make_async_copy(pack2, r.K2.at[rows8, :], r.s_small.at[1]).start()
    pltpu.make_async_copy(lrp.at[f], r.LR.at[rows8, :], r.s_small.at[2]).start()

    def send_small(k):
        g = (f + k) & (nf - 1)
        dev = (blk, g)
        remote(lrp.at[g], r.LR.at[rows8, :], r.s_small_tx.at[2], r.s_small.at[2], dev).start()
        remote(pack1, r.K1.at[:, :, cols], r.s_small_tx.at[0], r.s_small.at[0], dev).start()
        remote(pack2, r.K2.at[rows8, :], r.s_small_tx.at[1], r.s_small.at[1], dev).start()

    lax.fori_loop(1, nf, lambda k, c: (send_small(k), c)[1], 0)

    def weight_src(l, a):
        return [w_shared.at[l], w_pair.at[l, 0], w_pair.at[l, 1], w_out.at[l]][a]

    def weight_dst(l, a, g, count=1):
        if a == 0:
            m = D // nf
            return r.Ws.at[l, pl.ds(pl.multiple_of(g * m, m), m * count), :]
        if a == 3:
            return r.Wo.at[l, pl.ds(pl.multiple_of(g * cw, cw), cw * count), :]
        return (r.Wv if a == 1 else r.Wg).at[l, :, pl.ds(pl.multiple_of(g * cw, cw), cw * count)]

    sibling = (blk, x * 2 + 1 - core)

    way = 1 - 2 * core

    def peer(dx):
        return (blk, ((x + nx + dx) & (nx - 1)) * 2 + core)

    def shard_of(dx):
        return ((x + nx + dx) & (nx - 1)) * 2 + core

    def weights_send(l, arrays):
        for a in arrays:
            mine = weight_dst(l, a, f)
            src, tx = weight_src(l, a), r.s_w_tx.at[l, a]
            pltpu.make_async_copy(src, mine, r.s_wloc.at[l, a]).start()
            remote(src, mine, tx, r.s_w.at[l, a, 0], peer(way)).start()
            remote(src, mine, tx, r.s_w.at[l, a, 1], peer(-way)).start()
            remote(src, mine, tx, r.s_sib.at[l, a], sibling).start()

    def weights_pass(l, a, i, dx, relay):
        part = weight_dst(l, a, shard_of(dx))
        arrived(part, r.s_w.at[l, a, i])
        if relay:
            remote(part, part, r.s_w_tx.at[l, a], r.s_w.at[l, a, 2], peer(way)).start()
        remote(part, part, r.s_w_tx.at[l, a], r.s_sib.at[l, a], sibling).start()

    def weights_relay(l, arrays):
        for a in arrays:
            weights_pass(l, a, 0, -way, True)
            weights_pass(l, a, 1, way, False)

    def weights_last(l, arrays):
        for a in arrays:
            weights_pass(l, a, 2, 2, False)

    def weights_wait(l, arrays):
        for a in arrays:
            pltpu.make_async_copy(weight_src(l, a), weight_dst(l, a, f), r.s_wloc.at[l, a]).wait()
            arrived(weight_dst(l, a, 0, nx), r.s_sib.at[l, a])

    weights_send(0, (0, 1, 2, 3))

    def expand(v, l, at):
        hi = v.astype(BF)
        rest = v - hi.astype(F32)
        mid = rest.astype(BF)
        lo = (rest - mid.astype(F32)).astype(BF)
        e = r.E[l, :, at]
        return mm(hi, e) + mm(mid, e) + mm(lo, e)

    arrived(r.LR, r.s_small.at[2])
    upper = jnp.where(iota((T, T), 0) <= iota((T, T), 1), 1.0, 0.0)
    cum = jnp.dot(r.LR[...], upper, preferred_element_type=F32, precision=lax.Precision.HIGHEST)
    cum_t = jnp.transpose(cum)
    spans = [expand(cum_t[T - 8 :, :], l, slice(None))[7:8, :] for l in range(2)]
    r.SPS[...] = jnp.where(iota((8, HP), 0) < 4, spans[0], spans[1])

    def lanes_of(q):
        return pl.ds(pl.multiple_of((q >> nf_bits) * lw, lw), lw)

    def rows_of(q):
        return pl.ds(pl.multiple_of((q & (nf - 1)) * ar, ar), ar)

    pltpu.make_async_copy(r.SPS.at[:, lanes_of(me)], r.SPR.at[me], r.s_sp.at[0]).start()

    def send_span(k):
        q = (me + k) & (np_ - 1)
        remote(r.SPS.at[:, lanes_of(q)], r.SPR.at[me], r.s_sp_tx.at[0], r.s_sp.at[0], plane(q)).start()

    lax.fori_loop(1, np_, lambda k, c: (send_span(k), c)[1], 0)

    ecum = jnp.exp(cum_t)
    remain = jnp.exp(cum_t[T - 1 :, :] - cum_t)
    for l in range(2):
        for j in range(4):
            at = pl.ds(j * 256, 256)
            r.EC[l, :, at] = expand(ecum, l, at)
            r.RM[l, :, at] = expand(remain, l, at)
    causal = iota((T, T), 0) >= iota((T, T), 1)
    anti = iota((T, T), 0) <= iota((T, T), 1)
    for l in range(2):
        for h in range(H):
            s = slot(l, h)
            down, along = cum_t[:, s : s + 1], cum[s : s + 1, :]
            r.DM[l, h] = jnp.exp(jnp.where(causal, down - along, -1e30)).astype(BF)
            r.DTM[l, h] = jnp.exp(jnp.where(anti, along - down, -1e30)).astype(BF)

    arrived(r.K1, r.s_small.at[0])
    arrived(r.K2, r.s_small.at[1])
    r.WST[...] = r.K2[:, :D].astype(BF)
    bias_t = jnp.transpose(r.K2[:, D:])
    r.BIAS[...] = bias_t[:8, :]
    def plane_spans():
        arrived(r.SPR, r.s_sp.at[0])

        def take_span(p, total):
            tile = r.SPR[p]
            r.EA[0, p] = jnp.broadcast_to(jnp.exp(tile[0:1, :]), (ar, lw))
            r.EA[1, p] = jnp.broadcast_to(jnp.exp(tile[4:5, :]), (ar, lw))
            return total + tile

        r.ZS[...] = lax.fori_loop(0, np_, take_span, jnp.zeros((8, lw), F32))
        pltpu.make_async_copy(r.ZS, r.ZR.at[z], r.s_sp.at[1]).start()

        def send_zspan(k):
            other = (z + k) & (nz - 1)
            remote(r.ZS, r.ZR.at[z], r.s_sp_tx.at[1], r.s_sp.at[1], (other * ny + y, f)).start()

        lax.fori_loop(1, nz, lambda k, c: (send_zspan(k), c)[1], 0)

    def world_spans():
        arrived(r.ZR, r.s_sp.at[1])

        def take_zspan(p):
            tile = r.ZR[p]
            r.EZ[0, p] = jnp.broadcast_to(jnp.exp(tile[0:1, :]), (ar, lw))
            r.EZ[1, p] = jnp.broadcast_to(jnp.exp(tile[4:5, :]), (ar, lw))

        loop(nz, take_zspan)

    def chain_send(s, yy, first):
        def one(k, c):
            g = (f + k) & (nf - 1)
            rows = pl.ds(pl.multiple_of(g * ar, ar), ar)
            at = pl.ds(pl.multiple_of(yy * lw, lw), lw)
            remote(
                r.CL.at[s, rows, at], r.R1.at[s, me], r.s_a_tx.at[s], r.s_a.at[s], (z * ny + yy, g)
            ).start()
            return c

        lax.fori_loop(first, nf, one, 0)

    def chain_quarters(s, make):
        def one(j, c):
            yy = (y + j) & (ny - 1)
            make(yy)
            chain_send(s, yy, 0)
            return c

        lax.fori_loop(1, ny, one, 0, unroll=True)
        make(y)
        pltpu.make_async_copy(r.CL.at[s, rows_of(me), lanes_of(me)], r.R1.at[s, me], r.s_a.at[s]).start()
        chain_send(s, y, 1)

    def chain_take(s, use):
        def one(j, c):
            yy = (y + ny - j) & (ny - 1)
            arrived(r.OP.at[s, :, pl.ds(pl.multiple_of(yy * lw, lw), lw)], r.s_b.at[s, yy])
            use(yy)
            return c

        lax.fori_loop(1, ny + 1, one, 0, unroll=True)

    def chain_planes(s, l, rev):
        arrived(r.R1.at[s], r.s_a.at[s])

        def add(k, t):
            p = np_ - 1 - k if rev else k
            return r.EA[l, p] * t + r.R1[s, p].astype(F32)

        total = lax.fori_loop(0, np_, add, jnp.zeros((ar, lw), F32), unroll=8)
        r.ZT[s] = total.astype(BF)
        pltpu.make_async_copy(r.ZT.at[s], r.RZ.at[s, z], r.s_z.at[s]).start()

        def one(k, c):
            other = (z + k) & (nz - 1)
            remote(r.ZT.at[s], r.RZ.at[s, z], r.s_z_tx.at[s], r.s_z.at[s], (other * ny + y, f)).start()
            return c

        lax.fori_loop(1, nz, one, 0)

    def chain_return(s, l, rev):
        arrived(r.RZ.at[s], r.s_z.at[s])

        def over(k, o):
            p = nz - 1 - k if rev else k
            new = r.EZ[l, p] * o + r.RZ[s, p].astype(F32)
            return jnp.where((p > z) if rev else (p < z), new, o)

        o = lax.fori_loop(0, nz, over, jnp.zeros((ar, lw), F32), unroll=True)

        def each(k, o):
            p = np_ - 1 - k if rev else k
            r.SB[s, p] = o.astype(BF)
            return r.EA[l, p] * o + r.R1[s, p].astype(F32)

        lax.fori_loop(0, np_, each, o, unroll=8)
        mine = r.OP.at[s, rows_of(me), lanes_of(me)]
        pltpu.make_async_copy(r.SB.at[s, me], mine, r.s_b.at[s, y]).start()

        def one(k, c):
            q = (me + k) & (np_ - 1)
            remote(r.SB.at[s, q], mine, r.s_b_tx.at[s], r.s_b.at[s, y], plane(q)).start()
            return c

        lax.fori_loop(1, np_, one, 0)

    def taps(l, k, j):
        if j is None:
            return conv_shared[l, k : k + 1, :]
        return r.K1[l, k : k + 1, j]

    def quarter(j):
        return pl.ds(pl.multiple_of(j * 256, 256), 256)

    def eighth(j):
        return pl.ds(pl.multiple_of(j * 128, 128), 128)

    tail = pl.ds(HP, 2 * N)
    left = iota((T, 128), 1) < HEAD

    def stacked(v):
        return jnp.concatenate([jnp.where(left, v, 0.0), jnp.where(left, 0.0, v)], axis=0).astype(BF)

    def forward(l, cur):
        r.CUR[l] = cur
        scale = lax.rsqrt(jnp.mean(cur * cur, axis=-1, keepdims=True) + EPS)
        r.HID[...] = (cur * scale * in_gain[l : l + 1, :]).astype(BF)
        weights_wait(l, (0, 1))
        r.BEF[l, 8:, tail] = mm(r.HID[...], r.Ws[l]).astype(BF).astype(F32)

        def values(j):
            at = quarter(j)
            r.BEF[l, 8:, at] = mm(r.HID[...], r.Wv[l, :, at]).astype(BF).astype(F32)

        loop(4, values)
        rim = r.BEF.at[l, pl.ds(0, 8), :]
        remote(r.BEF.at[l, pl.ds(T, 8), :], rim, r.s_rim_tx.at[l], r.s_rim.at[l], dev_after).start()
        if l == 0:
            weights_relay(0, (2, 3))
            weights_last(0, (2,))
            weights_send(1, (2, 3))
        weights_wait(l, (2,))

        def gates(j):
            at = quarter(j)
            g = mm(r.HID[...], r.Wg[l, :, at]).astype(BF).astype(F32)
            sig = sigmoid(g)
            r.SG[:, at] = g * sig
            r.DSG[:, at] = sig * (1.0 + g * (1.0 - sig))

        loop(4, gates)
        pre = mmt(r.HID[...], r.WST[...]) + r.BIAS[0:1, :]
        r.SGM[l] = sigmoid(pre)
        step = jnp.maximum(pre, 0.0) + jnp.log1p(jnp.exp(-jnp.abs(pre)))
        hi = step.astype(BF)
        lo = (step - hi.astype(F32)).astype(BF)

        def steps(j):
            at = quarter(j)
            e = r.E[l, :, at]
            r.ST[l, :, at] = mm(hi, e) + mm(lo, e)

        loop(4, steps)
        arrived(rim, r.s_rim.at[l])

        @pl.when(seq == 0)
        def _():
            r.BEF[l, 0:8, :] = jnp.zeros((8, AC), F32)

        def conv(at, j):
            total = taps(l, 0, j) * r.BEF[l, 5 : 5 + T, at]
            for k in range(1, 4):
                total = total + taps(l, k, j) * r.BEF[l, 5 + k : 5 + k + T, at]
            sig = sigmoid(total)
            act = (total * sig).astype(BF)
            r.ACT[l, :, at] = act
            r.DSIL[l, :, at] = sig * (1.0 + total * (1.0 - sig))
            return act.astype(F32)

        bc = conv(tail, None)
        b_t = jnp.transpose(bc[:, :N]).astype(BF)
        r.BT[...] = b_t
        r.CT[l] = jnp.transpose(bc[:, N:]).astype(BF)
        b, c = bc[:, :N].astype(BF), bc[:, N:].astype(BF)
        r.SS[...] = mmt(c, b)
        r.STT[l] = mmt(b, c)

        def inputs(j):
            at = quarter(j)
            act = conv(at, at)
            xs = act * r.ST[l, :, at]
            wx = (xs * r.RM[l, :, at]).astype(BF)
            r.XS[l, :, at] = xs.astype(BF)
            r.WX[l, :, at] = wx
            r.CL[l, :, at] = mm(r.BT[...], wx).astype(BF)

        chain_quarters(l, inputs)
        if l == 0:
            weights_last(0, (3,))
            plane_spans()

        def within(j):
            at = eighth(j)
            scores = r.SS[...]
            m = jnp.concatenate(
                [(r.DM[l, 2 * j].astype(F32) * scores).astype(BF), (r.DM[l, 2 * j + 1].astype(F32) * scores).astype(BF)],
                axis=1,
            )
            skip = r.K1[l, 5:6, at]
            r.Y[:, at] = mm(m, stacked(r.XS[l, :, at].astype(F32))) + skip * r.ACT[l, :, at].astype(F32)

        loop(4, within)
        chain_planes(l, l, False)
        lax.fori_loop(4, 8, lambda j, c: (within(j), c)[1], 0, unroll=True)
        if l == 0:
            weights_relay(1, (0, 1, 2, 3))
            world_spans()
        chain_return(l, l, False)
        if l == 0:
            weights_last(1, (0, 1, 2, 3))
        weights_wait(l, (3,))

        def finish(j):
            at = quarter(j)
            yy = r.Y[:, at] + r.EC[l, :, at] * mm(r.ACT[l, :, pl.ds(HP + N, N)], r.OP[l, :, at])
            gated = yy * r.SG[:, at]
            rr = lax.rsqrt(mm((gated * gated).astype(BF), r.J[...]) + EPS)
            gn = gated * rr
            r.GN[l, :, at] = gn
            r.HO[:, at] = (gn * r.K1[l, 4:5, at]).astype(BF)
            r.RSG[l, :, at] = rr * r.SG[:, at]
            r.RYD[l, :, at] = rr * yy * r.DSG[:, at]

        chain_take(l, finish)
        return (r.CUR[l] + mm(r.HO[...], r.Wo[l])).astype(BF)

    def backward(l):
        s = 3 - l
        u = r.U[...].astype(BF)
        c_t = r.CT[l]

        def enter(j):
            at = quarter(j)
            dn = mmt(u, r.Wo[l, at, :]) * r.K1[l, 4:5, at]
            gn = r.GN[l, :, at]
            t = dn - gn * mm((dn * gn).astype(BF), r.J[...])
            dy = t * r.RSG[l, :, at]
            r.DY[:, at] = dy
            r.DGA[:, at] = (t * r.RYD[l, :, at]).astype(BF)
            q = (r.EC[l, :, at] * dy).astype(BF)
            r.Q[:, at] = q
            r.CL[s, :, at] = mm(c_t, q).astype(BF)

        chain_quarters(s, enter)
        r.DS[...] = jnp.zeros((T, T), F32)

        def within(j):
            at = eighth(j)
            dy2 = stacked(r.DY[:, at])
            dm = mmt(dy2, r.XS[l, :, at])
            r.DS[...] += r.DM[l, 2 * j].astype(F32) * dm[:T] + r.DM[l, 2 * j + 1].astype(F32) * dm[T:]
            turned = r.STT[l]
            m_t = jnp.concatenate(
                [(r.DTM[l, 2 * j].astype(F32) * turned).astype(BF), (r.DTM[l, 2 * j + 1].astype(F32) * turned).astype(BF)],
                axis=1,
            )
            r.DXS[:, at] = mm(m_t, dy2)

        loop(4, within)
        chain_planes(s, l, True)
        if l == 1:
            publish_relay(0, mixed_o)
        lax.fori_loop(4, 8, lambda j, c: (within(j), c)[1], 0, unroll=True)
        b, c = r.ACT[l, :, pl.ds(HP, N)], r.ACT[l, :, pl.ds(HP + N, N)]
        ds = r.DS[...]
        r.DBC[:, N:] = mm(ds.astype(BF), b) + mmt(r.Q[...], r.OP[l])
        r.DBC[:, :N] = mm(jnp.transpose(ds).astype(BF), c)
        chain_return(s, l, True)
        if l == 1:
            publish_last(0, mixed_o)
        r.DST[...] = jnp.zeros((T, slots), F32)

        def leave(j):
            at = quarter(j)
            b = r.ACT[l, :, pl.ds(HP, N)]
            g = r.OP[s, :, at]
            r.DBC[:, :N] += mmt(r.WX[l, :, at], g)
            dxs = r.DXS[:, at] + r.RM[l, :, at] * mm(b, g)
            act = r.ACT[l, :, at].astype(F32)
            dx = dxs * r.ST[l, :, at] + r.K1[l, 5:6, at] * r.DY[:, at]
            r.DST[...] += mm((dxs * act).astype(BF), r.ET[l, at, :])
            r.DTOT[l, 0:T, at] = dx.astype(BF).astype(F32) * r.DSIL[l, :, at]

        chain_take(s, leave)
        r.DTOT[l, 0:T, tail] = r.DBC[...].astype(BF).astype(F32) * r.DSIL[l, :, tail]
        rim = r.DTOT.at[l, pl.ds(T, 8), :]
        remote(r.DTOT.at[l, pl.ds(0, 8), :], rim, r.s_rim_tx.at[s], r.s_rim.at[s], dev_ahead).start()
        r.DH[...] = mmt(r.DGA[...], r.Wg[l]) + mm((r.DST[...] * r.SGM[l]).astype(BF), r.WST[...])
        arrived(rim, r.s_rim.at[s])

        @pl.when(seq == nseq - 1)
        def _():
            r.DTOT[l, T:, :] = jnp.zeros((8, AC), F32)

        def unconv(at, j):
            total = taps(l, 0, j) * r.DTOT[l, 3 : 3 + T, at]
            for k in range(1, 4):
                total = total + taps(l, k, j) * r.DTOT[l, 3 - k : 3 - k + T, at]
            r.DB[:, at] = total.astype(BF)

        unconv(tail, None)
        loop(4, lambda j: unconv(quarter(j), quarter(j)))
        dn = r.DH[...] + mmt(r.DB[:, :HP], r.Wv[l]) + mmt(r.DB[:, HP:], r.Ws[l])
        cur = r.CUR[l]
        scale = lax.rsqrt(jnp.mean(cur * cur, axis=-1, keepdims=True) + EPS)
        dg = dn * in_gain[l : l + 1, :]
        dcur = scale * dg - cur * (scale * scale * scale * jnp.mean(cur * dg, axis=-1, keepdims=True))
        return (r.U[...] + dcur).astype(BF)

    def rows_at(g):
        return pl.ds(pl.multiple_of(g * T, T), T)

    def publish(i, staged, out):
        tx = r.s_out_tx.at[i]
        pltpu.make_async_copy(staged, out.at[own, :], r.s_out_own.at[i]).start()
        remote(staged, out.at[own, :], tx, r.s_out.at[i, 0], peer(way)).start()
        remote(staged, out.at[own, :], tx, r.s_out.at[i, 1], peer(-way)).start()
        remote(staged, out.at[own, :], tx, r.s_out_sib.at[i], sibling).start()

    def publish_pass(i, out, k, dx, relay):
        part = out.at[rows_at(shard_of(dx)), :]
        arrived(part, r.s_out.at[i, k])
        if relay:
            remote(part, part, r.s_out_tx.at[i], r.s_out.at[i, 2], peer(way)).start()
        remote(part, part, r.s_out_tx.at[i], r.s_out_sib.at[i], sibling).start()

    def publish_relay(i, out):
        publish_pass(i, out, 0, -way, True)
        publish_pass(i, out, 1, way, False)

    def publish_last(i, out):
        publish_pass(i, out, 2, 2, False)

    weights_relay(0, (0, 1))
    weights_last(0, (0, 1))
    weights_send(1, (0, 1))
    in_tok.wait()
    stream = forward(0, r.TOK[...].astype(F32))
    stream = forward(1, stream.astype(F32))
    r.MIXS[...] = stream
    publish(0, r.MIXS, mixed_o)
    in_cot.wait()
    r.U[...] = r.COT[...].astype(F32)
    r.U[...] = backward(1).astype(F32)
    r.GRS[...] = backward(0)
    publish(1, r.GRS, grad_o)
    publish_relay(1, grad_o)
    publish_last(1, grad_o)

    some = pl.ds(0, (nf - 1) * R2)
    arrived(r.K1.at[:, :, pl.ds(0, (nf - 1) * cw)], r.s_small_tx.at[0])
    arrived(r.K2.at[some, :], r.s_small_tx.at[1])
    arrived(r.LR.at[some, :], r.s_small_tx.at[2])
    for l in range(2):
        for a in range(4):
            arrived(weight_dst(l, a, 0, nf - 1), r.s_w_tx.at[l, a])
    arrived(r.SPR.at[pl.ds(0, np_ - 1)], r.s_sp_tx.at[0])
    arrived(r.ZR.at[pl.ds(0, nz - 1)], r.s_sp_tx.at[1])
    for s in range(4):
        arrived(r.R1.at[s, pl.ds(0, np_ - 1)], r.s_a_tx.at[s])
        arrived(r.RZ.at[s, pl.ds(0, nz - 1)], r.s_z_tx.at[s])
        arrived(r.SB.at[s, pl.ds(0, np_ - 1)], r.s_b_tx.at[s])
        arrived(r.BEF.at[0, pl.ds(0, 8), :], r.s_rim_tx.at[s])
    for i, out in enumerate((mixed_o, grad_o)):
        arrived(out.at[pl.ds(0, (nf - 1) * T), :], r.s_out_tx.at[i])
        arrived(out.at[pl.ds(0, nx * T), :], r.s_out_sib.at[i])
        arrived(out.at[own, :], r.s_out_own.at[i])


def body(nb, nf, *args):
    (tokens, cotangent, in_gain, w_pair, w_shared, w_step, step_bias, conv_values, conv_shared, log_decay,
     skip_gain, out_gain, w_out) = args
    steps = jnp.transpose(w_step, (0, 2, 1)).astype(F32)
    parts = layout(nb, nf)
    vmem, hbm = pl.BlockSpec(memory_space=pltpu.VMEM), pl.BlockSpec(memory_space=pl.ANY)
    shape = jax.ShapeDtypeStruct(tokens.shape, BF)
    return pl.pallas_call(
        functools.partial(kernel, nb, nf, tuple(parts)),
        out_shape=(pltpu.VMEM(tokens.shape, BF), pltpu.VMEM(tokens.shape, BF)),
        in_specs=[hbm, hbm, vmem, hbm, hbm, hbm] + [vmem] * 7,
        out_specs=(hbm, hbm),
        scratch_shapes=list(parts.values()),
        compiler_params=pltpu.CompilerParams(has_side_effects=True, collective_id=0, vmem_limit_bytes=56 * 2**20),
        name="layers",
    )(tokens, cotangent, in_gain, w_pair, w_shared, w_out, conv_values, out_gain, skip_gain, steps, step_bias, log_decay,
      conv_shared)


def solution(mesh):
    nb, nf = mesh.shape["blk"], mesh.shape["fsdp"]
    in_specs = (
        P("blk", None),
        P("blk", None),
        P(),
        P(None, None, None, "fsdp"),
        P(None, "fsdp", None),
        P(None, None, "fsdp"),
        P(None, "fsdp"),
        P(None, None, "fsdp"),
        P(),
        P(None, "fsdp", "blk"),
        P(None, "fsdp"),
        P(None, "fsdp"),
        P(None, "fsdp", None),
    )
    out_specs = (P("blk", None), P("blk", None))
    return jax.shard_map(
        functools.partial(body, nb, nf), mesh=mesh, in_specs=in_specs, out_specs=out_specs, check_vma=False
    )
```

```python
import functools

import jax
import jax.numpy as jnp
from jax import lax
from jax.experimental import pallas as pl
from jax.experimental.pallas import tpu as pltpu
from jax.sharding import PartitionSpec as P

D = 512
H = 16
HEAD = 64
N = 128
T = 128
HP = H * HEAD
AC = HP + 2 * N
EPS = 1e-5
PY = 4
R2 = 8
F32, BF = jnp.float32, jnp.bfloat16
MESH = pl.DeviceIdType.MESH


def mm(a, b):
    return jnp.dot(a, b, preferred_element_type=F32)


def mmt(a, b):
    return lax.dot_general(a, b, (((1,), (1,)), ((), ())), preferred_element_type=F32)


def sigmoid(v):
    return 1.0 / (1.0 + jnp.exp(-v))


def iota(shape, dim):
    return lax.broadcasted_iota(jnp.int32, shape, dim)


def loop(count, fn):
    def step(i, carry):
        fn(i)
        return carry

    lax.fori_loop(0, count, step, 0, unroll=True)


def layout(nb, nf):
    ny, nz = PY, nb // PY
    np_ = ny * nf
    ar, lw = N // nf, HP // ny
    slots = nf * R2
    hf = H // nf
    vm = pltpu.VMEM
    dma = pltpu.SemaphoreType.DMA
    return dict(
        Wv=vm((2, D, HP), BF), Wg=vm((2, D, HP), BF), Wo=vm((2, HP, D), BF), Ws=vm((2, D, 2 * N), BF),
        K1=vm((2, 8, HP), F32), K2=vm((slots, D + 128), F32), LR=vm((slots, T), F32),
        WST=vm((slots, D), BF), BIAS=vm((8, slots), F32), E=vm((2, slots, HP), BF), ET=vm((2, HP, slots), BF),
        J=vm((256, 256), BF), EC=vm((2, T, HP), F32), RM=vm((2, T, HP), F32),
        DM=vm((2, H, T, T), BF), DTM=vm((2, H, T, T), BF),
        SPS=vm((8, HP), F32), SPR=vm((np_, 8, lw), F32), EA=vm((2, np_, ar, lw), F32),
        ZS=vm((8, lw), F32), ZR=vm((nz, 8, lw), F32), EZ=vm((2, nz, ar, lw), F32),
        TOK=vm((T, D), BF), COT=vm((T, D), BF), MIXS=vm((T, D), BF), GRS=vm((T, D), BF),
        CUR=vm((2, T, D), F32), HID=vm((T, D), BF), BEF=vm((2, T + 8, AC), F32), DSIL=vm((2, T, AC), F32),
        ACT=vm((2, T, AC), BF), ST=vm((2, T, HP), F32), SGM=vm((2, T, slots), F32),
        XS=vm((2, T, HP), BF), WX=vm((2, T, HP), BF), BT=vm((N, T), BF), CT=vm((2, N, T), BF),
        SS=vm((T, T), F32), STT=vm((2, T, T), F32), SG=vm((T, HP), F32), DSG=vm((T, HP), F32), Y=vm((T, HP), F32),
        HO=vm((T, HP), BF), GN=vm((2, T, HP), F32), RSG=vm((2, T, HP), F32), RYD=vm((2, T, HP), F32),
        CL=vm((4, N, HP), BF), R1=vm((4, np_, ar, lw), BF), ZT=vm((4, ar, lw), BF), RZ=vm((4, nz, ar, lw), BF),
        SB=vm((4, np_, ar, lw), BF), OP=vm((4, N, HP), BF),
        DY=vm((T, HP), F32), Q=vm((T, HP), BF), DGA=vm((T, HP), BF), DXS=vm((T, HP), F32), DS=vm((T, T), F32),
        DBC=vm((T, 2 * N), F32), DST=vm((T, slots), F32), DTOT=vm((2, T + 8, AC), F32), DB=vm((T, AC), BF),
        DH=vm((T, D), F32), U=vm((T, D), F32),
        P1=vm((2, 8, hf * HEAD), F32), P2=vm((R2, D + 128), F32), P3=vm((nf, R2, T), F32), s_in=dma((2,)), s_small=dma((3,)), s_small_tx=dma((3,)), s_w=dma((2, 4, 3)), s_sib=dma((2, 4)), s_wloc=dma((2, 4)),
        s_w_tx=dma((2, 4)), s_sp=dma((2,)), s_sp_tx=dma((2,)), s_rim=dma((4,)), s_rim_tx=dma((4,)),
        s_a=dma((4,)), s_a_tx=dma((4,)), s_z=dma((4,)), s_z_tx=dma((4,)), s_b=dma((4, ny)), s_b_tx=dma((4,)),
        s_out=dma((2, 3)), s_out_sib=dma((2,)), s_out_own=dma((2,)), s_out_tx=dma((2,)),
    )


class Refs:
    pass


def kernel(nb, nf, names, *refs):
    (tokens, cot, in_gain, w_pair, w_shared, w_out, conv_values, out_gain, skip_gain, steps, step_bias, rates,
     conv_shared, mixed_o, grad_o) = refs[:15]
    r = Refs()
    for name, ref in zip(names, refs[15:]):
        setattr(r, name, ref)
    ny, nz = PY, nb // PY
    np_ = ny * nf
    ar, lw = N // nf, HP // ny
    slots = nf * R2
    hf = H // nf
    hf_bits = hf.bit_length() - 1
    cw = HP // nf
    nx = nf // 2
    blk, f = lax.axis_index("blk"), lax.axis_index("fsdp")
    ny_bits, nf_bits = ny.bit_length() - 1, nf.bit_length() - 1
    z, y = blk >> ny_bits, blk & (ny - 1)
    me = y * nf + f
    x, core = f >> 1, f & 1

    def plane(q):
        return (z * ny + (q >> nf_bits), q & (nf - 1))

    def remote(src, dst, tx, rx, dev):
        return pltpu.make_async_remote_copy(
            src_ref=src, dst_ref=dst, send_sem=tx, recv_sem=rx, device_id=dev, device_id_type=MESH
        )

    def arrived(ref, sem):
        pltpu.make_async_copy(ref, ref, sem).wait()

    def slot(l, h):
        return (h // hf) * R2 + l * hf + h % hf

    seq = blk * nf + f
    nseq = nb * nf
    after, ahead = (seq + 1) & (nseq - 1), (seq + nseq - 1) & (nseq - 1)
    dev_after = (after >> nf_bits, after & (nf - 1))
    dev_ahead = (ahead >> nf_bits, ahead & (nf - 1))

    barrier = pltpu.get_barrier_semaphore()

    def greet(dev):
        pl.semaphore_signal(barrier, inc=1, device_id=dev, device_id_type=MESH)

    lax.fori_loop(1, np_, lambda k, c: (greet(plane((me + k) & (np_ - 1))), c)[1], 0)
    lax.fori_loop(1, nz, lambda k, c: (greet((((z + k) & (nz - 1)) * ny + y, f)), c)[1], 0)

    @pl.when(me == np_ - 1)
    def _():
        greet(dev_after)

    @pl.when(me == 0)
    def _():
        greet(dev_ahead)

    own = pl.ds(pl.multiple_of(f * T, T), T)
    in_tok = pltpu.make_async_copy(tokens.at[own, :], r.TOK, r.s_in.at[0])
    in_cot = pltpu.make_async_copy(cot.at[own, :], r.COT, r.s_in.at[1])
    in_tok.start()
    in_cot.start()

    for l in range(2):
        s_at = iota((slots, HP), 0)
        head = iota((slots, HP), 1) >> 6
        want = (head >> hf_bits) * R2 + l * hf + (head & (hf - 1))
        r.E[l] = jnp.where(s_at == want, 1.0, 0.0).astype(BF)
        s_at = iota((HP, slots), 1)
        head = iota((HP, slots), 0) >> 6
        want = (head >> hf_bits) * R2 + l * hf + (head & (hf - 1))
        r.ET[l] = jnp.where(s_at == want, 1.0, 0.0).astype(BF)
    r.J[...] = jnp.where((iota((256, 256), 0) >> 6) == (iota((256, 256), 1) >> 6), 1.0 / HEAD, 0.0).astype(BF)

    pack1, pack2, lrp = r.P1, r.P2, r.P3
    if hf * 2 < R2:
        pack2[...] = jnp.zeros((R2, D + 128), F32)
        lrp[...] = jnp.zeros((nf, R2, T), F32)
    for l in range(2):
        pack1[l, 0:4, :] = conv_values[l]
        pack1[l, 4:5, :] = out_gain[l : l + 1, :]
        for h in range(hf):
            pack1[l, 5:6, h * HEAD : (h + 1) * HEAD] = jnp.broadcast_to(skip_gain[l : l + 1, h : h + 1], (1, HEAD))
            row = l * hf + h
            pack2[row : row + 1, D:] = jnp.broadcast_to(step_bias[l : l + 1, h : h + 1], (1, 128))
            pack2[row : row + 1, :D] = steps[l, h : h + 1, :]
            for g in range(nf):
                lrp[g, row : row + 1, :] = rates[l, h : h + 1, g * T : (g + 1) * T]
        pack1[l, 6:8, :] = jnp.zeros((2, hf * HEAD), F32)
    rim_peer = jnp.where(jnp.logical_or(me == 0, me == np_ - 1), 1, 0)
    pl.semaphore_wait(barrier, np_ + nz - 2 + rim_peer)
    cols = pl.ds(pl.multiple_of(f * cw, cw), cw)
    rows8 = pl.ds(pl.multiple_of(f * R2, R2), R2)
    pltpu.make_async_copy(pack1, r.K1.at[:, :, cols], r.s_small.at[0]).start()
    pltpu.make_async_copy(pack2, r.K2.at[rows8, :], r.s_small.at[1]).start()
    pltpu.make_async_copy(lrp.at[f], r.LR.at[rows8, :], r.s_small.at[2]).start()

    def send_small(k):
        g = (f + k) & (nf - 1)
        dev = (blk, g)
        remote(lrp.at[g], r.LR.at[rows8, :], r.s_small_tx.at[2], r.s_small.at[2], dev).start()
        remote(pack1, r.K1.at[:, :, cols], r.s_small_tx.at[0], r.s_small.at[0], dev).start()
        remote(pack2, r.K2.at[rows8, :], r.s_small_tx.at[1], r.s_small.at[1], dev).start()

    lax.fori_loop(1, nf, lambda k, c: (send_small(k), c)[1], 0)

    def weight_src(l, a):
        return [w_shared.at[l], w_pair.at[l, 0], w_pair.at[l, 1], w_out.at[l]][a]

    def weight_dst(l, a, g, count=1):
        if a == 0:
            m = D // nf
            return r.Ws.at[l, pl.ds(pl.multiple_of(g * m, m), m * count), :]
        if a == 3:
            return r.Wo.at[l, pl.ds(pl.multiple_of(g * cw, cw), cw * count), :]
        return (r.Wv if a == 1 else r.Wg).at[l, :, pl.ds(pl.multiple_of(g * cw, cw), cw * count)]

    sibling = (blk, x * 2 + 1 - core)

    way = 1 - 2 * core

    def peer(dx):
        return (blk, ((x + nx + dx) & (nx - 1)) * 2 + core)

    def shard_of(dx):
        return ((x + nx + dx) & (nx - 1)) * 2 + core

    def weights_send(l, arrays):
        for a in arrays:
            mine = weight_dst(l, a, f)
            src, tx = weight_src(l, a), r.s_w_tx.at[l, a]
            pltpu.make_async_copy(src, mine, r.s_wloc.at[l, a]).start()
            remote(src, mine, tx, r.s_w.at[l, a, 0], peer(way)).start()
            remote(src, mine, tx, r.s_w.at[l, a, 1], peer(-way)).start()
            remote(src, mine, tx, r.s_sib.at[l, a], sibling).start()

    def weights_pass(l, a, i, dx, relay):
        part = weight_dst(l, a, shard_of(dx))
        arrived(part, r.s_w.at[l, a, i])
        if relay:
            remote(part, part, r.s_w_tx.at[l, a], r.s_w.at[l, a, 2], peer(way)).start()
        remote(part, part, r.s_w_tx.at[l, a], r.s_sib.at[l, a], sibling).start()

    def weights_relay(l, arrays):
        for a in arrays:
            weights_pass(l, a, 0, -way, True)
            weights_pass(l, a, 1, way, False)

    def weights_last(l, arrays):
        for a in arrays:
            weights_pass(l, a, 2, 2, False)

    def weights_wait(l, arrays):
        for a in arrays:
            pltpu.make_async_copy(weight_src(l, a), weight_dst(l, a, f), r.s_wloc.at[l, a]).wait()
            arrived(weight_dst(l, a, 0, nx), r.s_sib.at[l, a])

    weights_send(0, (0, 1, 2, 3))

    def expand(v, l, at):
        hi = v.astype(BF)
        rest = v - hi.astype(F32)
        mid = rest.astype(BF)
        lo = (rest - mid.astype(F32)).astype(BF)
        e = r.E[l, :, at]
        return mm(hi, e) + mm(mid, e) + mm(lo, e)

    arrived(r.LR, r.s_small.at[2])
    upper = jnp.where(iota((T, T), 0) <= iota((T, T), 1), 1.0, 0.0)
    cum = jnp.dot(r.LR[...], upper, preferred_element_type=F32, precision=lax.Precision.HIGHEST)
    cum_t = jnp.transpose(cum)
    spans = [expand(cum_t[T - 8 :, :], l, slice(None))[7:8, :] for l in range(2)]
    r.SPS[...] = jnp.where(iota((8, HP), 0) < 4, spans[0], spans[1])

    def lanes_of(q):
        return pl.ds(pl.multiple_of((q >> nf_bits) * lw, lw), lw)

    def rows_of(q):
        return pl.ds(pl.multiple_of((q & (nf - 1)) * ar, ar), ar)

    pltpu.make_async_copy(r.SPS.at[:, lanes_of(me)], r.SPR.at[me], r.s_sp.at[0]).start()

    def send_span(k):
        q = (me + k) & (np_ - 1)
        remote(r.SPS.at[:, lanes_of(q)], r.SPR.at[me], r.s_sp_tx.at[0], r.s_sp.at[0], plane(q)).start()

    lax.fori_loop(1, np_, lambda k, c: (send_span(k), c)[1], 0)

    ecum = jnp.exp(cum_t)
    remain = jnp.exp(cum_t[T - 1 :, :] - cum_t)
    for l in range(2):
        for j in range(4):
            at = pl.ds(j * 256, 256)
            r.EC[l, :, at] = expand(ecum, l, at)
            r.RM[l, :, at] = expand(remain, l, at)
    causal = iota((T, T), 0) >= iota((T, T), 1)
    anti = iota((T, T), 0) <= iota((T, T), 1)
    for l in range(2):
        for h in range(H):
            s = slot(l, h)
            down, along = cum_t[:, s : s + 1], cum[s : s + 1, :]
            r.DM[l, h] = jnp.exp(jnp.where(causal, down - along, -1e30)).astype(BF)
            r.DTM[l, h] = jnp.exp(jnp.where(anti, along - down, -1e30)).astype(BF)

    arrived(r.K1, r.s_small.at[0])
    arrived(r.K2, r.s_small.at[1])
    r.WST[...] = r.K2[:, :D].astype(BF)
    bias_t = jnp.transpose(r.K2[:, D:])
    r.BIAS[...] = bias_t[:8, :]
    def plane_spans():
        arrived(r.SPR, r.s_sp.at[0])

        def take_span(p, total):
            tile = r.SPR[p]
            r.EA[0, p] = jnp.broadcast_to(jnp.exp(tile[0:1, :]), (ar, lw))
            r.EA[1, p] = jnp.broadcast_to(jnp.exp(tile[4:5, :]), (ar, lw))
            return total + tile

        r.ZS[...] = lax.fori_loop(0, np_, take_span, jnp.zeros((8, lw), F32))
        pltpu.make_async_copy(r.ZS, r.ZR.at[z], r.s_sp.at[1]).start()

        def send_zspan(k):
            other = (z + k) & (nz - 1)
            remote(r.ZS, r.ZR.at[z], r.s_sp_tx.at[1], r.s_sp.at[1], (other * ny + y, f)).start()

        lax.fori_loop(1, nz, lambda k, c: (send_zspan(k), c)[1], 0)

    def world_spans():
        arrived(r.ZR, r.s_sp.at[1])

        def take_zspan(p):
            tile = r.ZR[p]
            r.EZ[0, p] = jnp.broadcast_to(jnp.exp(tile[0:1, :]), (ar, lw))
            r.EZ[1, p] = jnp.broadcast_to(jnp.exp(tile[4:5, :]), (ar, lw))

        loop(nz, take_zspan)

    def chain_send(s, yy, first):
        def one(k, c):
            g = (f + k) & (nf - 1)
            rows = pl.ds(pl.multiple_of(g * ar, ar), ar)
            at = pl.ds(pl.multiple_of(yy * lw, lw), lw)
            remote(
                r.CL.at[s, rows, at], r.R1.at[s, me], r.s_a_tx.at[s], r.s_a.at[s], (z * ny + yy, g)
            ).start()
            return c

        lax.fori_loop(first, nf, one, 0)

    def chain_quarters(s, make):
        def one(j, c):
            yy = (y + j) & (ny - 1)
            make(yy)
            chain_send(s, yy, 0)
            return c

        lax.fori_loop(1, ny, one, 0, unroll=True)
        make(y)
        pltpu.make_async_copy(r.CL.at[s, rows_of(me), lanes_of(me)], r.R1.at[s, me], r.s_a.at[s]).start()
        chain_send(s, y, 1)

    def chain_take(s, use):
        def one(j, c):
            yy = (y + ny - j) & (ny - 1)
            arrived(r.OP.at[s, :, pl.ds(pl.multiple_of(yy * lw, lw), lw)], r.s_b.at[s, yy])
            use(yy)
            return c

        lax.fori_loop(1, ny + 1, one, 0, unroll=True)

    def chain_planes(s, l, rev):
        arrived(r.R1.at[s], r.s_a.at[s])

        def add(k, t):
            p = np_ - 1 - k if rev else k
            return r.EA[l, p] * t + r.R1[s, p].astype(F32)

        total = lax.fori_loop(0, np_, add, jnp.zeros((ar, lw), F32), unroll=8)
        r.ZT[s] = total.astype(BF)
        pltpu.make_async_copy(r.ZT.at[s], r.RZ.at[s, z], r.s_z.at[s]).start()

        def one(k, c):
            other = (z + k) & (nz - 1)
            remote(r.ZT.at[s], r.RZ.at[s, z], r.s_z_tx.at[s], r.s_z.at[s], (other * ny + y, f)).start()
            return c

        lax.fori_loop(1, nz, one, 0)

    def chain_return(s, l, rev):
        arrived(r.RZ.at[s], r.s_z.at[s])

        def over(k, o):
            p = nz - 1 - k if rev else k
            new = r.EZ[l, p] * o + r.RZ[s, p].astype(F32)
            return jnp.where((p > z) if rev else (p < z), new, o)

        o = lax.fori_loop(0, nz, over, jnp.zeros((ar, lw), F32), unroll=True)

        def each(k, o):
            p = np_ - 1 - k if rev else k
            r.SB[s, p] = o.astype(BF)
            return r.EA[l, p] * o + r.R1[s, p].astype(F32)

        lax.fori_loop(0, np_, each, o, unroll=8)
        mine = r.OP.at[s, rows_of(me), lanes_of(me)]
        pltpu.make_async_copy(r.SB.at[s, me], mine, r.s_b.at[s, y]).start()

        def one(k, c):
            q = (me + k) & (np_ - 1)
            remote(r.SB.at[s, q], mine, r.s_b_tx.at[s], r.s_b.at[s, y], plane(q)).start()
            return c

        lax.fori_loop(1, np_, one, 0)

    def taps(l, k, j):
        if j is None:
            return conv_shared[l, k : k + 1, :]
        return r.K1[l, k : k + 1, j]

    def quarter(j):
        return pl.ds(pl.multiple_of(j * 256, 256), 256)

    def eighth(j):
        return pl.ds(pl.multiple_of(j * 128, 128), 128)

    tail = pl.ds(HP, 2 * N)
    left = iota((T, 128), 1) < HEAD

    def stacked(v):
        return jnp.concatenate([jnp.where(left, v, 0.0), jnp.where(left, 0.0, v)], axis=0).astype(BF)

    def forward(l, cur):
        r.CUR[l] = cur
        scale = lax.rsqrt(jnp.mean(cur * cur, axis=-1, keepdims=True) + EPS)
        r.HID[...] = (cur * scale * in_gain[l : l + 1, :]).astype(BF)
        weights_wait(l, (0, 1))
        r.BEF[l, 8:, tail] = mm(r.HID[...], r.Ws[l]).astype(BF).astype(F32)

        def values(j):
            at = quarter(j)
            r.BEF[l, 8:, at] = mm(r.HID[...], r.Wv[l, :, at]).astype(BF).astype(F32)

        loop(4, values)
        rim = r.BEF.at[l, pl.ds(0, 8), :]
        remote(r.BEF.at[l, pl.ds(T, 8), :], rim, r.s_rim_tx.at[l], r.s_rim.at[l], dev_after).start()
        if l == 0:
            weights_relay(0, (2, 3))
            weights_last(0, (2,))
            weights_send(1, (2, 3))
        weights_wait(l, (2,))

        def gates(j):
            at = quarter(j)
            g = mm(r.HID[...], r.Wg[l, :, at]).astype(BF).astype(F32)
            sig = sigmoid(g)
            r.SG[:, at] = g * sig
            r.DSG[:, at] = sig * (1.0 + g * (1.0 - sig))

        loop(4, gates)
        pre = mmt(r.HID[...], r.WST[...]) + r.BIAS[0:1, :]
        r.SGM[l] = sigmoid(pre)
        step = jnp.maximum(pre, 0.0) + jnp.log1p(jnp.exp(-jnp.abs(pre)))
        hi = step.astype(BF)
        lo = (step - hi.astype(F32)).astype(BF)

        def steps(j):
            at = quarter(j)
            e = r.E[l, :, at]
            r.ST[l, :, at] = mm(hi, e) + mm(lo, e)

        loop(4, steps)
        arrived(rim, r.s_rim.at[l])

        @pl.when(seq == 0)
        def _():
            r.BEF[l, 0:8, :] = jnp.zeros((8, AC), F32)

        def conv(at, j):
            total = taps(l, 0, j) * r.BEF[l, 5 : 5 + T, at]
            for k in range(1, 4):
                total = total + taps(l, k, j) * r.BEF[l, 5 + k : 5 + k + T, at]
            sig = sigmoid(total)
            act = (total * sig).astype(BF)
            r.ACT[l, :, at] = act
            r.DSIL[l, :, at] = sig * (1.0 + total * (1.0 - sig))
            return act.astype(F32)

        bc = conv(tail, None)
        b_t = jnp.transpose(bc[:, :N]).astype(BF)
        r.BT[...] = b_t
        r.CT[l] = jnp.transpose(bc[:, N:]).astype(BF)
        b, c = bc[:, :N].astype(BF), bc[:, N:].astype(BF)
        r.SS[...] = mmt(c, b)
        r.STT[l] = mmt(b, c)

        def inputs(j):
            at = quarter(j)
            act = conv(at, at)
            xs = act * r.ST[l, :, at]
            wx = (xs * r.RM[l, :, at]).astype(BF)
            r.XS[l, :, at] = xs.astype(BF)
            r.WX[l, :, at] = wx
            r.CL[l, :, at] = mm(r.BT[...], wx).astype(BF)

        chain_quarters(l, inputs)
        if l == 0:
            weights_last(0, (3,))
            weights_relay(1, (0, 1))
            plane_spans()

        def within(j):
            at = eighth(j)
            scores = r.SS[...]
            m = jnp.concatenate(
                [(r.DM[l, 2 * j].astype(F32) * scores).astype(BF), (r.DM[l, 2 * j + 1].astype(F32) * scores).astype(BF)],
                axis=1,
            )
            skip = r.K1[l, 5:6, at]
            r.Y[:, at] = mm(m, stacked(r.XS[l, :, at].astype(F32))) + skip * r.ACT[l, :, at].astype(F32)

        loop(4, within)
        chain_planes(l, l, False)
        lax.fori_loop(4, 8, lambda j, c: (within(j), c)[1], 0, unroll=True)
        if l == 0:
            weights_relay(1, (2, 3))
            weights_last(1, (0, 1))
            world_spans()
        chain_return(l, l, False)
        if l == 0:
            weights_last(1, (2, 3))
        weights_wait(l, (3,))

        def finish(j):
            at = quarter(j)
            yy = r.Y[:, at] + r.EC[l, :, at] * mm(r.ACT[l, :, pl.ds(HP + N, N)], r.OP[l, :, at])
            gated = yy * r.SG[:, at]
            rr = lax.rsqrt(mm((gated * gated).astype(BF), r.J[...]) + EPS)
            gn = gated * rr
            r.GN[l, :, at] = gn
            r.HO[:, at] = (gn * r.K1[l, 4:5, at]).astype(BF)
            r.RSG[l, :, at] = rr * r.SG[:, at]
            r.RYD[l, :, at] = rr * yy * r.DSG[:, at]

        chain_take(l, finish)
        return (r.CUR[l] + mm(r.HO[...], r.Wo[l])).astype(BF)

    def backward(l):
        s = 3 - l
        u = r.U[...].astype(BF)
        c_t = r.CT[l]

        def enter(j):
            at = quarter(j)
            dn = mmt(u, r.Wo[l, at, :]) * r.K1[l, 4:5, at]
            gn = r.GN[l, :, at]
            t = dn - gn * mm((dn * gn).astype(BF), r.J[...])
            dy = t * r.RSG[l, :, at]
            r.DY[:, at] = dy
            r.DGA[:, at] = (t * r.RYD[l, :, at]).astype(BF)
            q = (r.EC[l, :, at] * dy).astype(BF)
            r.Q[:, at] = q
            r.CL[s, :, at] = mm(c_t, q).astype(BF)

        chain_quarters(s, enter)
        r.DS[...] = jnp.zeros((T, T), F32)

        def within(j):
            at = eighth(j)
            dy2 = stacked(r.DY[:, at])
            dm = mmt(dy2, r.XS[l, :, at])
            r.DS[...] += r.DM[l, 2 * j].astype(F32) * dm[:T] + r.DM[l, 2 * j + 1].astype(F32) * dm[T:]
            turned = r.STT[l]
            m_t = jnp.concatenate(
                [(r.DTM[l, 2 * j].astype(F32) * turned).astype(BF), (r.DTM[l, 2 * j + 1].astype(F32) * turned).astype(BF)],
                axis=1,
            )
            r.DXS[:, at] = mm(m_t, dy2)

        loop(4, within)
        chain_planes(s, l, True)
        if l == 1:
            publish_relay(0, mixed_o)
        lax.fori_loop(4, 8, lambda j, c: (within(j), c)[1], 0, unroll=True)
        b, c = r.ACT[l, :, pl.ds(HP, N)], r.ACT[l, :, pl.ds(HP + N, N)]
        ds = r.DS[...]
        r.DBC[:, N:] = mm(ds.astype(BF), b) + mmt(r.Q[...], r.OP[l])
        r.DBC[:, :N] = mm(jnp.transpose(ds).astype(BF), c)
        chain_return(s, l, True)
        if l == 1:
            publish_last(0, mixed_o)
        r.DST[...] = jnp.zeros((T, slots), F32)

        def leave(j):
            at = quarter(j)
            b = r.ACT[l, :, pl.ds(HP, N)]
            g = r.OP[s, :, at]
            r.DBC[:, :N] += mmt(r.WX[l, :, at], g)
            dxs = r.DXS[:, at] + r.RM[l, :, at] * mm(b, g)
            act = r.ACT[l, :, at].astype(F32)
            dx = dxs * r.ST[l, :, at] + r.K1[l, 5:6, at] * r.DY[:, at]
            r.DST[...] += mm((dxs * act).astype(BF), r.ET[l, at, :])
            r.DTOT[l, 0:T, at] = dx.astype(BF).astype(F32) * r.DSIL[l, :, at]

        chain_take(s, leave)
        r.DTOT[l, 0:T, tail] = r.DBC[...].astype(BF).astype(F32) * r.DSIL[l, :, tail]
        rim = r.DTOT.at[l, pl.ds(T, 8), :]
        remote(r.DTOT.at[l, pl.ds(0, 8), :], rim, r.s_rim_tx.at[s], r.s_rim.at[s], dev_ahead).start()
        r.DH[...] = mmt(r.DGA[...], r.Wg[l]) + mm((r.DST[...] * r.SGM[l]).astype(BF), r.WST[...])
        arrived(rim, r.s_rim.at[s])

        @pl.when(seq == nseq - 1)
        def _():
            r.DTOT[l, T:, :] = jnp.zeros((8, AC), F32)

        def unconv(at, j):
            total = taps(l, 0, j) * r.DTOT[l, 3 : 3 + T, at]
            for k in range(1, 4):
                total = total + taps(l, k, j) * r.DTOT[l, 3 - k : 3 - k + T, at]
            r.DB[:, at] = total.astype(BF)

        unconv(tail, None)
        loop(4, lambda j: unconv(quarter(j), quarter(j)))
        dn = r.DH[...] + mmt(r.DB[:, :HP], r.Wv[l]) + mmt(r.DB[:, HP:], r.Ws[l])
        cur = r.CUR[l]
        scale = lax.rsqrt(jnp.mean(cur * cur, axis=-1, keepdims=True) + EPS)
        dg = dn * in_gain[l : l + 1, :]
        dcur = scale * dg - cur * (scale * scale * scale * jnp.mean(cur * dg, axis=-1, keepdims=True))
        return (r.U[...] + dcur).astype(BF)

    def rows_at(g):
        return pl.ds(pl.multiple_of(g * T, T), T)

    def publish(i, staged, out):
        tx = r.s_out_tx.at[i]
        pltpu.make_async_copy(staged, out.at[own, :], r.s_out_own.at[i]).start()
        remote(staged, out.at[own, :], tx, r.s_out.at[i, 0], peer(way)).start()
        remote(staged, out.at[own, :], tx, r.s_out.at[i, 1], peer(-way)).start()
        remote(staged, out.at[own, :], tx, r.s_out_sib.at[i], sibling).start()

    def publish_pass(i, out, k, dx, relay):
        part = out.at[rows_at(shard_of(dx)), :]
        arrived(part, r.s_out.at[i, k])
        if relay:
            remote(part, part, r.s_out_tx.at[i], r.s_out.at[i, 2], peer(way)).start()
        remote(part, part, r.s_out_tx.at[i], r.s_out_sib.at[i], sibling).start()

    def publish_relay(i, out):
        publish_pass(i, out, 0, -way, True)
        publish_pass(i, out, 1, way, False)

    def publish_last(i, out):
        publish_pass(i, out, 2, 2, False)

    weights_relay(0, (0, 1))
    weights_last(0, (0, 1))
    weights_send(1, (0, 1))
    in_tok.wait()
    stream = forward(0, r.TOK[...].astype(F32))
    stream = forward(1, stream.astype(F32))
    r.MIXS[...] = stream
    publish(0, r.MIXS, mixed_o)
    in_cot.wait()
    r.U[...] = r.COT[...].astype(F32)
    r.U[...] = backward(1).astype(F32)
    r.GRS[...] = backward(0)
    publish(1, r.GRS, grad_o)
    publish_relay(1, grad_o)
    publish_last(1, grad_o)

    some = pl.ds(0, (nf - 1) * R2)
    arrived(r.K1.at[:, :, pl.ds(0, (nf - 1) * cw)], r.s_small_tx.at[0])
    arrived(r.K2.at[some, :], r.s_small_tx.at[1])
    arrived(r.LR.at[some, :], r.s_small_tx.at[2])
    for l in range(2):
        for a in range(4):
            arrived(weight_dst(l, a, 0, nf - 1), r.s_w_tx.at[l, a])
    arrived(r.SPR.at[pl.ds(0, np_ - 1)], r.s_sp_tx.at[0])
    arrived(r.ZR.at[pl.ds(0, nz - 1)], r.s_sp_tx.at[1])
    for s in range(4):
        arrived(r.R1.at[s, pl.ds(0, np_ - 1)], r.s_a_tx.at[s])
        arrived(r.RZ.at[s, pl.ds(0, nz - 1)], r.s_z_tx.at[s])
        arrived(r.SB.at[s, pl.ds(0, np_ - 1)], r.s_b_tx.at[s])
        arrived(r.BEF.at[0, pl.ds(0, 8), :], r.s_rim_tx.at[s])
    for i, out in enumerate((mixed_o, grad_o)):
        arrived(out.at[pl.ds(0, (nf - 1) * T), :], r.s_out_tx.at[i])
        arrived(out.at[pl.ds(0, nx * T), :], r.s_out_sib.at[i])
        arrived(out.at[own, :], r.s_out_own.at[i])


def body(nb, nf, *args):
    (tokens, cotangent, in_gain, w_pair, w_shared, w_step, step_bias, conv_values, conv_shared, log_decay,
     skip_gain, out_gain, w_out) = args
    steps = jnp.transpose(w_step, (0, 2, 1)).astype(F32)
    parts = layout(nb, nf)
    vmem, hbm = pl.BlockSpec(memory_space=pltpu.VMEM), pl.BlockSpec(memory_space=pl.ANY)
    shape = jax.ShapeDtypeStruct(tokens.shape, BF)
    return pl.pallas_call(
        functools.partial(kernel, nb, nf, tuple(parts)),
        out_shape=(pltpu.VMEM(tokens.shape, BF), pltpu.VMEM(tokens.shape, BF)),
        in_specs=[hbm, hbm, vmem, hbm, hbm, hbm] + [vmem] * 7,
        out_specs=(hbm, hbm),
        scratch_shapes=list(parts.values()),
        compiler_params=pltpu.CompilerParams(has_side_effects=True, collective_id=0, vmem_limit_bytes=56 * 2**20),
        name="layers",
    )(tokens, cotangent, in_gain, w_pair, w_shared, w_out, conv_values, out_gain, skip_gain, steps, step_bias, log_decay,
      conv_shared)


def solution(mesh):
    nb, nf = mesh.shape["blk"], mesh.shape["fsdp"]
    in_specs = (
        P("blk", None),
        P("blk", None),
        P(),
        P(None, None, None, "fsdp"),
        P(None, "fsdp", None),
        P(None, None, "fsdp"),
        P(None, "fsdp"),
        P(None, None, "fsdp"),
        P(),
        P(None, "fsdp", "blk"),
        P(None, "fsdp"),
        P(None, "fsdp"),
        P(None, "fsdp", None),
    )
    out_specs = (P("blk", None), P("blk", None))
    return jax.shard_map(
        functools.partial(body, nb, nf), mesh=mesh, in_specs=in_specs, out_specs=out_specs, check_vma=False
    )
```
